32 devices in a mesh: gx: 8 (over z, y), gy: 4 (over x, core).
Axes of the slice: x: 2, y: 2, z: 4, core: 2. Of those that a mesh axis runs over, the one named last changes fastest.
Arguments:
- density: float32 [256, 128, 512], P('gx', 'gy'), may hold values from 0.5 to 2
- momentum: float32 [3, 256, 128, 512], P(None, 'gx', 'gy'), may hold values from -3 to 3
- energy: float32 [256, 128, 512], P('gx', 'gy'), may hold values from 2 to 4
- coarse_rows: float32 [2, 2048, 4, 160], P(None, 'gx', 'gy'), may hold values from -2 to 4, as said below
- ghost_rows: int32 [4, 8, 128], P('gy'), may hold values from 0 to 2047, as said below
- time_index: int32 [4, 8, 128], P('gy'), may hold values from 0 to 8
Outputs:
- section_state: float32 [5, 256, 128, 512], P(None, 'gx', 'gy')
The draws below stay inside these ranges and needn't reach their ends.
Inputs may be any that keep to these rules, and one draw needn't show every extreme that they name: `ghost_rows`: entry [b, a, s] names a coarse row of column b; rows c * 256 to (c + 1) * 256 - 1 of a column lie on the device with gx index c. Exactly 16 of one device's slots name rows held by each source device. `coarse_rows`: field 0 of every row (density) lies in 0.5 to 2.
All inputs are finite; a program needn't handle non-finite values.
Results may differ from the reference program's by a relative error of at most 0.0003.
Values sent between devices are 32-bit elements; how exact they have to be, the bound alone decides.
A program may use at most 256 MiB of HBM per device.

```python
import jax
import jax.numpy as jnp
from jax import lax

CXY = 32
CZ = 512
CROW = 256
NX = 256
NY = 128
COARSE_ROWS = 2048
GHOST_SLOTS = 128
N_GX = 8
N_GY = 4


def draw_coarse_rows(key, part):
    key_rho = jax.random.fold_in(key, 11)
    key_mom = jax.random.fold_in(key, 12)
    key_ene = jax.random.fold_in(key, 13)
    rho_part = jax.random.uniform(key_rho, (2, COARSE_ROWS, N_GY, 1, CXY), jnp.float32, 0.5, 2.0)
    mom_part = jnp.clip(0.5 * jax.random.normal(key_mom, (2, COARSE_ROWS, N_GY, 3, CXY), jnp.float32), -2.0, 2.0)
    ene_part = jax.random.uniform(key_ene, (2, COARSE_ROWS, N_GY, 1, CXY), jnp.float32, 2.0, 4.0)
    joined = jnp.concatenate([rho_part, mom_part, ene_part], axis=3)
    return joined.reshape(2, COARSE_ROWS, N_GY, 5 * CXY).astype(jnp.float32)


def draw_ghost_rows(key, part):
    capacity = 4 * CXY // N_GX
    base_device = jax.random.randint(jax.random.fold_in(key, 21), (N_GY, N_GX, 1), 0, N_GX)
    row_offset = jax.random.randint(jax.random.fold_in(key, 22), (N_GY, N_GX, 4 * CXY), 0, CROW)
    slot_ids = jnp.arange(4 * CXY, dtype=jnp.int32)
    side_of = slot_ids // (2 * CXY)
    within = slot_ids % (2 * CXY)
    offset_src = jnp.where(side_of >= 1, N_GX // 2, 0)
    source = (base_device + offset_src + within // capacity) % N_GX
    return (source * CROW + row_offset).astype(jnp.int32)


def place_ends(values, stream_key, low, largest):
    longest = values.shape.index(max(values.shape))
    spots = []
    for shift in (0, 1):
        where = [jax.random.randint(jax.random.fold_in(stream_key, axis), (), 0, length) for axis, length in enumerate(values.shape)]
        where[longest] = (where[longest] + shift) % values.shape[longest]
        spots.append(tuple(where))
    return values.at[spots[0]].set(low).at[spots[1]].set(largest)


def levels(key, dims, pieces, least, high):
    level = 1.0
    for dim, blocks in pieces:
        heights = jax.random.uniform(jax.random.fold_in(jax.random.fold_in(key, 6), dim), (blocks,), jnp.float32, least / len(pieces), high / len(pieces))
        level = level * jnp.repeat(jnp.exp(heights), dims[dim] // blocks).reshape((-1,) + (1,) * (len(dims) - 1 - dim))
    return level


def normal_values(stream_key, dims, spread, reach, pieces=(), held_as=jnp.bfloat16):
    drawn = jax.random.normal(stream_key, dims, jnp.float32) * spread
    if len(pieces) > 0:
        drawn = levels(stream_key, dims, pieces, -0.22, 0.18) * drawn
    return jnp.clip(drawn, min=-reach, max=reach).astype(held_as)


def setup_inputs(seed: int = 0) -> dict:
    splits = jax.random.split(jax.random.key(seed), 7)
    density = jnp.clip(0.5 + 1.5 * jax.random.uniform(splits[0], (NX, NY, CZ), jnp.float32) ** levels(splits[0], (NX, NY, CZ), ((0, 8), (1, 4)), -0.2, 0.2), 0.5, 2.0)
    momentum = normal_values(splits[1], (3, NX, NY, CZ), 0.5, 3.0, ((1, 8), (2, 4)), jnp.float32)
    energy = jnp.clip(2.0 + 2.0 * jax.random.uniform(splits[2], (NX, NY, CZ), jnp.float32) ** levels(splits[2], (NX, NY, CZ), ((0, 8), (1, 4)), -0.2, 0.2), 2.0, 4.0)
    coarse_rows = draw_coarse_rows(jax.random.fold_in(splits[6], 71), 0)
    ghost_rows = draw_ghost_rows(jax.random.fold_in(splits[6], 71), 0)
    time_index = place_ends(jax.random.randint(splits[5], (N_GY, N_GX, GHOST_SLOTS), 0, 9), jax.random.fold_in(splits[5], 1), 0, 8).astype(jnp.int32)
    return dict(density=density, momentum=momentum, energy=energy, coarse_rows=coarse_rows, ghost_rows=ghost_rows, time_index=time_index)


beta_coef = 1.0 / 3.0
a_coef = 14.0 / 9.0
b_coef = 1.0 / 9.0
gamma_gas = 1.4
time_step = 0.4

def fluxes(fields, direction):
    density = fields[0]
    carried = fields[1 + direction]
    velocity = carried / density
    kinetic = (fields[1] * fields[1] + fields[2] * fields[2] + fields[3] * fields[3]) / density
    pressure = (gamma_gas - 1.0) * (fields[4] - 0.5 * kinetic)
    columns = [carried]
    for component in range(3):
        product_term = fields[1 + component] * velocity
        if component == direction:
            product_term = product_term + pressure
        columns.append(product_term)
    columns.append((fields[4] + pressure) * velocity)
    return jnp.stack(columns)

def stencil(extended, line_axis, length):

    def window(offset):
        return lax.slice_in_dim(extended, offset, offset + length, axis=line_axis)
    return 0.5 * a_coef * (window(3) - window(1)) + 0.25 * b_coef * (window(4) - window(0))

def interpolate(coarse_column, row_ids, level_index):
    safe_rows = jnp.maximum(row_ids, 0)
    picked_old = coarse_column[0][safe_rows]
    picked_new = coarse_column[1][safe_rows]
    weight = (level_index.astype(jnp.float32) * 0.125)[..., None]
    blended = (1.0 - weight) * picked_old + weight * picked_new
    return jnp.where((row_ids >= 0)[..., None], blended, 0.0)

def ghost_layers(coarse_rows, ghost_rows, time_index):
    values = jax.vmap(interpolate, in_axes=(2, 0, 0))(coarse_rows, ghost_rows, time_index)
    values = values.reshape(N_GY, N_GX, 4, CXY, 5, CXY).transpose(4, 1, 3, 0, 5, 2)
    return values.reshape(5, NX, NY, 4)

def solve_lines(right, line_axis):
    length = right.shape[line_axis]
    positions = jnp.arange(length)
    distance = jnp.abs(positions[:, None] - positions[None, :])
    matrix = jnp.where(distance == 0, 1.0, jnp.where(distance == 1, beta_coef, 0.0)).astype(jnp.float32)
    moved = jnp.moveaxis(right, line_axis, 0)
    flattened = moved.reshape(length, -1)
    solved = jnp.linalg.solve(matrix, flattened)
    return jnp.moveaxis(solved.reshape(moved.shape), 0, line_axis)

def reference(density, momentum, energy, coarse_rows, ghost_rows, time_index):
    fields = jnp.concatenate([density[None], momentum, energy[None]], axis=0)
    layers = ghost_layers(coarse_rows, ghost_rows, time_index)
    extended_z = jnp.concatenate([layers[..., 0:2], fields, layers[..., 2:4]], axis=3)
    flux_x = jnp.pad(fluxes(fields, 0), ((0, 0), (2, 2), (0, 0), (0, 0)))
    flux_y = jnp.pad(fluxes(fields, 1), ((0, 0), (0, 0), (2, 2), (0, 0)))
    flux_z = fluxes(extended_z, 2)
    deriv_x = solve_lines(stencil(flux_x, 1, NX), 1)
    deriv_y = solve_lines(stencil(flux_y, 2, NY), 2)
    deriv_z = solve_lines(stencil(flux_z, 3, CZ), 3)
    return fields - time_step * (deriv_x + deriv_y + deriv_z)
```

```python
import functools

import jax
import jax.numpy as jnp
import numpy as np
from jax import lax
from jax.experimental import pallas as pl
from jax.experimental.pallas import tpu as pltpu
from jax.sharding import PartitionSpec as P

beta_coef = 1.0 / 3.0
near_coef = 7.0 / 9.0
far_coef = 1.0 / 36.0
time_step = 0.4
highest = lax.Precision.HIGHEST
vmem_bytes = 50 * 1024 * 1024


def line_matrices(length):
    matrix = np.eye(length) + beta_coef * (np.eye(length, k=1) + np.eye(length, k=-1))
    rows = np.arange(length)
    spread = np.zeros((length, length + 4))
    spread[rows, rows + 3] += near_coef
    spread[rows, rows + 1] -= near_coef
    spread[rows, rows + 4] += far_coef
    spread[rows, rows] -= far_coef
    return np.linalg.inv(matrix), spread


def split_table(table):
    table = np.asarray(table, np.float32)
    high = table.astype(jnp.bfloat16)
    return high, (table - high.astype(np.float32)).astype(jnp.bfloat16)


def block_tables(cells, groups):
    length = cells * groups
    inverse, spread = line_matrices(length)
    whole = -time_step * inverse @ spread[:, 2:-2]
    own = np.zeros((groups, cells, cells))
    beyond = np.zeros((groups, 4, cells))
    act = np.zeros((groups, 4, cells))
    for g in range(groups):
        s, e = g * cells, (g + 1) * cells
        own[g] = whole[s:e, s:e]
        if g > 0:
            beyond[g, 0] = whole[s - 1, s:e]
            beyond[g, 1] = whole[s - 2, s:e]
            act[g, 0, 0] = 1.0
            act[g, 1, 1:] = inverse[s + 1 : e, s] / inverse[s + 1, s]
        if g < groups - 1:
            beyond[g, 2] = whole[e, s:e]
            beyond[g, 3] = whole[e + 1, s:e]
            act[g, 2, cells - 1] = 1.0
            act[g, 3, : cells - 1] = inverse[s : e - 1, e - 1] / inverse[e - 2, e - 1]
    return own, beyond, act


def edge_scalars(beyond, cells):
    groups = beyond.shape[0]
    table = np.zeros((groups, 2 * cells + 4))
    table[:, :cells] = beyond[:, 1]
    table[:, cells : 2 * cells] = beyond[:, 3]
    for g in range(groups):
        if g > 0:
            table[g, 2 * cells] = beyond[g, 0, 1] / beyond[g, 1, 1]
            table[g, 2 * cells + 1] = beyond[g, 0, 0] - table[g, 2 * cells] * beyond[g, 1, 0]
        if g < groups - 1:
            table[g, 2 * cells + 2] = beyond[g, 2, cells - 2] / beyond[g, 3, cells - 2]
            table[g, 2 * cells + 3] = (
                beyond[g, 2, cells - 1] - table[g, 2 * cells + 2] * beyond[g, 3, cells - 1]
            )
    return table


def common(fields):
    rho, m1, m2, m3, energy = fields
    inv = 1.0 / rho
    pressure = 0.4 * (energy - 0.5 * inv * (m1 * m1 + m2 * m2 + m3 * m3))
    return inv, pressure, energy + pressure


def flux_from(fields, shared, direction):
    inv, pressure, total = shared
    velocity = fields[1 + direction] * inv
    out = [fields[1 + direction]]
    for component in range(3):
        term = fields[1 + component] * velocity
        out.append(term + pressure if component == direction else term)
    out.append(total * velocity)
    return out


def load_fields(rho, mom, ene, idx):
    return [rho[idx], mom[(0,) + idx], mom[(1,) + idx], mom[(2,) + idx], ene[idx]]


def store_split(high_ref, low_ref, idx, value):
    high = value.astype(jnp.bfloat16)
    high_ref[idx] = high
    low_ref[idx] = (value - high.astype(jnp.float32)).astype(jnp.bfloat16)


def dot3(left_hi, left_lo, right_hi, right_lo):
    dot = functools.partial(jnp.dot, preferred_element_type=jnp.float32)
    return dot(left_hi, right_hi) + dot(left_lo, right_hi) + dot(left_hi, right_lo)


def edge_kernel(
    place, cx, ey_hi, ey_lo, rho, mom, ene, xlo, xhi, ylo, yhi, g_hi, g_lo, *, cells, tile, last
):
    step = pl.program_id(0)
    px = place[0]
    zs = rho.shape[2] // 128
    pieces = cells // 16

    @pl.when(step == 0)
    def _():
        xlo[...] = jnp.zeros_like(xlo)
        xhi[...] = jnp.zeros_like(xhi)

    def piece(n, _):
        yy = pl.multiple_of((n // zs) * 16, 16)
        zz = pl.multiple_of((n % zs) * 128, 128)
        ys, zc = pl.ds(yy, 16), pl.ds(zz, 128)
        low = [xlo[f, 1, ys, zc] for f in range(5)]
        high = [xhi[f, 1, ys, zc] for f in range(5)]
        first = end = None
        for x in range(tile):
            fields = load_fields(rho, mom, ene, (x, ys, zc))
            shared = common(fields)
            flux = flux_from(fields, shared, 0)
            if x == 0:
                first = flux
            end = flux
            cl = cx[px, step * tile + x]
            ch = cx[px, cells + step * tile + x]
            for f in range(5):
                low[f] += cl * flux[f]
                high[f] += ch * flux[f]
            side = flux_from(fields, shared, 1)
            rows = pl.ds(pl.multiple_of(x * cells + yy, 16), 16)
            for f in range(5):
                store_split(g_hi, g_lo, (f, rows, zc), side[f])
        for f in range(5):
            xlo[f, 1, ys, zc] = low[f]
            xhi[f, 1, ys, zc] = high[f]

        @pl.when(step == 0)
        def _():
            for f in range(5):
                xlo[f, 0, ys, zc] = cx[px, 2 * cells + 1] * first[f]

        @pl.when(step == last)
        def _():
            for f in range(5):
                xlo[f, 0, ys, zc] += cx[px, 2 * cells] * low[f]
                xhi[f, 0, ys, zc] = cx[px, 2 * cells + 2] * high[f] + cx[px, 2 * cells + 3] * end[f]

        return 0

    lax.fori_loop(0, pieces * zs, piece, 0)
    for f in range(5):
        got = dot3(ey_hi[0], ey_lo[0], g_hi[f], g_lo[f])
        for e in range(2):
            ylo[f, e] = got[e * tile : (e + 1) * tile]
            yhi[f, e] = got[(2 + e) * tile : (3 + e) * tile]


def xline_kernel(place, mx_hi, mx_lo, rho, mom, ene, out, f_hi, f_lo, *, cells):
    zs = rho.shape[2] // 128
    half = cells // 4

    def piece(n, _):
        xx = (n // zs) * 4
        zc = pl.ds(pl.multiple_of((n % zs) * 128, 128), 128)
        fields = [v.reshape(32, 128) for v in load_fields(rho, mom, ene, (pl.ds(xx, 4), slice(None), zc))]
        flux = flux_from(fields, common(fields), 0)
        rows = pl.ds(pl.multiple_of(xx * 8, 32), 32)
        for f in range(5):
            store_split(f_hi, f_lo, (f, rows, zc), flux[f])
        return 0

    lax.fori_loop(0, half * zs, piece, 0)
    for f in range(5):
        got = dot3(mx_hi[0], mx_lo[0], f_hi[f], f_lo[f]).reshape(cells, 8, -1)
        base = rho[...] if f == 0 else ene[...] if f == 4 else mom[f - 1]
        out[f] = base + got


def yz_kernel(
    place, my_hi, my_lo, mz_hi, mz_lo, wz, hg, rho, mom, ene, acc, out, g_hi, g_lo, h_hi, h_lo, *, cells, tile
):
    zs = rho.shape[2] // 128

    def piece(n, _):
        x = n // zs
        zc = pl.ds(pl.multiple_of((n % zs) * 128, 128), 128)
        fields = load_fields(rho, mom, ene, (x, slice(None), zc))
        shared = common(fields)
        rows = pl.ds(pl.multiple_of(x * cells, 32), cells)
        for direction, hi, lo in ((1, g_hi, g_lo), (2, h_hi, h_lo)):
            flux = flux_from(fields, shared, direction)
            for f in range(5):
                store_split(hi, lo, (f, rows, zc), flux[f])
        return 0

    lax.fori_loop(0, tile * zs, piece, 0)
    for f in range(5):
        ends = lax.dot_general(
            hg[f], wz[...], (((0,), (0,)), ((), ())), precision=highest,
            preferred_element_type=jnp.float32,
        )
        got = (
            dot3(my_hi[0], my_lo[0], g_hi[f], g_lo[f])
            + dot3(h_hi[f], h_lo[f], mz_hi[...], mz_lo[...])
            + ends
        )
        out[f] = acc[f] + got.reshape(tile, cells, -1)


def join_kernel(place, ax, ay, acc, xlo, xhi, ylo, yhi, out, *, cells, tile):
    step = pl.program_id(0)
    px = place[0]
    zs = acc.shape[3] // 128

    def piece(n, _):
        zc = pl.ds(pl.multiple_of(n * 128, 128), 128)
        for x in range(tile):
            i = step * tile + x
            at_low = jnp.where(i == 0, 0, 1)
            at_high = jnp.where(i == cells - 1, 0, 1)
            cl, ch = ax[px, i], ax[px, cells + i]
            for f in range(5):
                term = acc[f, x, :, zc] + cl * xlo[f, at_low, :, zc] + ch * xhi[f, at_high, :, zc]
                for e in range(2):
                    term += ay[0, e] * ylo[f, e, x : x + 1, zc] + ay[0, 2 + e] * yhi[f, e, x : x + 1, zc]
                out[f, x, :, zc] = term
        return 0

    lax.fori_loop(0, zs, piece, 0)


def ghost_fluxes(coarse_rows, ghost_rows, time_index, groups_x, place_x, cells):
    slots = ghost_rows.shape[2]
    capacity = slots // groups_x
    block = coarse_rows.shape[1]
    rows = ghost_rows[0]
    weights = time_index[0].astype(jnp.float32) * 0.125
    mine = (rows // block == place_x).astype(jnp.int32)
    upper = (np.arange(slots)[:, None] <= np.arange(slots)[None, :]).astype(np.float32)
    rank = jnp.dot(mine.astype(jnp.float32), upper, precision=highest).astype(jnp.int32) - 1
    wanted = jnp.arange(capacity, dtype=jnp.int32)
    pick = (mine[:, None, :] > 0) & (rank[:, None, :] == wanted[None, :, None])
    local_rows = jnp.sum(jnp.where(pick, (rows - place_x * block)[:, None, :], 0), axis=2).reshape(-1)
    level = jnp.sum(jnp.where(pick, weights[:, None, :], 0.0), axis=2).reshape(-1, 1)
    onehot = (local_rows[:, None] == jnp.arange(block)[None, :]).astype(jnp.float32)
    old = jnp.dot(onehot, coarse_rows[0, :, 0, :], precision=highest)
    new = jnp.dot(onehot, coarse_rows[1, :, 0, :], precision=highest)
    sent = ((1.0 - level) * old + level * new).reshape(groups_x, capacity, -1)
    got = lax.all_to_all(sent, "gx", split_axis=0, concat_axis=0, tiled=True).reshape(slots, -1)
    owner = lax.dynamic_index_in_dim(rows, place_x, 0, keepdims=False) // block
    earlier = np.arange(slots)[None, :] < np.arange(slots)[:, None]
    nth = jnp.sum(((owner[:, None] == owner[None, :]) & earlier).astype(jnp.int32), axis=1)
    back = ((owner * capacity + nth)[:, None] == jnp.arange(slots)[None, :]).astype(jnp.float32)
    ghosts = jnp.dot(back, got, precision=highest).reshape(4, cells, 5, cells)
    fields = [ghosts[:, :, f] for f in range(5)]
    flux = jnp.stack(flux_from(fields, common(fields), 2)).reshape(5, 4, cells * cells)
    return jnp.pad(flux, ((0, 0), (0, 4), (0, 0)))


def local(density, momentum, energy, coarse_rows, ghost_rows, time_index):
    cells, _, cells_z = density.shape
    groups_x, groups_y = lax.axis_size("gx"), lax.axis_size("gy")
    place_x, place_y = lax.axis_index("gx"), lax.axis_index("gy")
    place = jnp.stack([place_x, place_y]).astype(jnp.int32)
    tile = 8
    steps = cells // tile
    f32 = jnp.float32

    own_x, beyond_x, act_x = block_tables(cells, groups_x)
    own_y, beyond_y, act_y = block_tables(cells, groups_y)
    inverse_z, spread_z = line_matrices(cells_z)
    whole_z = -time_step * inverse_z @ spread_z
    mx = split_table(np.stack([np.kron(m, np.eye(8)) for m in own_x]))
    my = split_table(np.stack([np.kron(np.eye(tile), m) for m in own_y]))
    ey = split_table(
        np.stack(
            [np.einsum("ej,xk->exkj", m, np.eye(tile)).reshape(4 * tile, tile * cells) for m in beyond_y]
        )
    )
    mz = split_table(whole_z[:, 2:-2].T)
    wz = np.zeros((8, cells_z), np.float32)
    wz[:4] = whole_z[:, [0, 1, cells_z + 2, cells_z + 3]].T
    cx = edge_scalars(beyond_x, cells).astype(np.float32)
    ax = np.concatenate([act_x[:, 0] + act_x[:, 1], act_x[:, 2] + act_x[:, 3]], axis=1).astype(np.float32)
    ay = np.broadcast_to(act_y[..., None], act_y.shape + (128,)).astype(np.float32)

    hg = ghost_fluxes(coarse_rows, ghost_rows, time_index, groups_x, place_x, cells)

    smem = pl.BlockSpec(memory_space=pltpu.SMEM)
    xtile3 = pl.BlockSpec((tile, cells, cells_z), lambda i, p: (i, 0, 0))
    xtile4 = pl.BlockSpec((3, tile, cells, cells_z), lambda i, p: (0, i, 0, 0))
    xtile5 = pl.BlockSpec((5, tile, cells, cells_z), lambda i, p: (0, i, 0, 0))
    xplane = pl.BlockSpec((5, 2, cells, cells_z), lambda i, p: (0, 0, 0, 0))
    yplane = pl.BlockSpec((5, 2, tile, cells_z), lambda i, p: (0, 0, i, 0))
    params = pltpu.CompilerParams(vmem_limit_bytes=vmem_bytes, dimension_semantics=("arbitrary",))
    planes = jax.ShapeDtypeStruct((5, 2, cells, cells_z), f32)
    whole = jax.ShapeDtypeStruct((5, cells, cells, cells_z), f32)

    def fixed(table, which=None):
        dims = table.shape[1:]
        if which is None:
            return pl.BlockSpec(table.shape, lambda i, p: (0,) * table.ndim)
        return pl.BlockSpec((1,) + dims, lambda i, p: (p[which],) + (0,) * len(dims))

    def call(kernel, in_specs, out_shape, out_specs, scratch, cost, **more):
        return pl.pallas_call(
            kernel,
            grid_spec=pltpu.PrefetchScalarGridSpec(
                num_scalar_prefetch=1, grid=(steps,), in_specs=in_specs, out_specs=out_specs,
                scratch_shapes=scratch,
            ),
            out_shape=out_shape,
            compiler_params=params,
            cost_estimate=pl.CostEstimate(flops=cost[0], bytes_accessed=cost[1], transcendentals=0),
            **more,
        )

    size = 4 * 5 * cells * cells * cells_z
    rows = tile * cells
    half = pltpu.VMEM((5, rows, cells_z), jnp.bfloat16)
    xlo, xhi, ylo, yhi = call(
        functools.partial(edge_kernel, cells=cells, tile=tile, last=steps - 1),
        [smem, fixed(ey[0], 1), fixed(ey[1], 1), xtile3, xtile4, xtile3],
        [planes] * 4,
        [xplane, xplane, yplane, yplane],
        [half, half],
        (size * 20, size),
        name="edges",
    )(place, cx, *ey, density, momentum, energy)

    def shift(array, axis, by):
        peers = lax.axis_size(axis)
        return lax.ppermute(
            array, axis, [(i, i + by) for i in range(peers) if 0 <= i + by < peers]
        )

    in_xlo = shift(xhi, "gx", 1)
    in_xhi = shift(xlo, "gx", -1)
    in_ylo = shift(yhi, "gy", 1)
    in_yhi = shift(ylo, "gy", -1)

    ytile3 = pl.BlockSpec((cells, 8, cells_z), lambda i, p: (0, i, 0))
    ytile4 = pl.BlockSpec((3, cells, 8, cells_z), lambda i, p: (0, 0, i, 0))
    ytile5 = pl.BlockSpec((5, cells, 8, cells_z), lambda i, p: (0, 0, i, 0))
    acc = call(
        functools.partial(xline_kernel, cells=cells),
        [fixed(mx[0], 0), fixed(mx[1], 0), ytile3, ytile4, ytile3],
        whole,
        ytile5,
        [half, half],
        (size * 400, 2 * size),
        name="xlines",
    )(place, *mx, density, momentum, energy)
    acc = call(
        functools.partial(yz_kernel, cells=cells, tile=tile),
        [
            fixed(my[0], 1), fixed(my[1], 1), fixed(mz[0]), fixed(mz[1]), fixed(wz),
            pl.BlockSpec((5, 8, rows), lambda i, p: (0, 0, i)), xtile3, xtile4, xtile3, xtile5,
        ],
        whole,
        xtile5,
        [half] * 4,
        (size * 1200, 3 * size),
        name="yzlines",
    )(place, *my, *mz, wz, hg, density, momentum, energy, acc)
    return call(
        functools.partial(join_kernel, cells=cells, tile=tile),
        [smem, fixed(ay, 1), xtile5, xplane, xplane, yplane, yplane],
        whole,
        xtile5,
        [],
        (size * 4, 2 * size),
        name="join",
    )(place, ax, ay, acc, in_xlo, in_xhi, in_ylo, in_yhi)


def solution(mesh):
    return jax.shard_map(
        local,
        mesh=mesh,
        in_specs=(
            P("gx", "gy", None),
            P(None, "gx", "gy", None),
            P("gx", "gy", None),
            P(None, "gx", "gy", None),
            P("gy", None, None),
            P("gy", None, None),
        ),
        out_specs=P(None, "gx", "gy", None),
        check_vma=False,
    )
```

```python
import functools

import jax
import jax.numpy as jnp
import numpy as np
from jax import lax
from jax.experimental import pallas as pl
from jax.experimental.pallas import tpu as pltpu
from jax.sharding import PartitionSpec as P

beta_coef = 1.0 / 3.0
near_coef = 7.0 / 9.0
far_coef = 1.0 / 36.0
time_step = 0.4
highest = lax.Precision.HIGHEST
vmem_bytes = 50 * 1024 * 1024


def line_matrices(length):
    matrix = np.eye(length) + beta_coef * (np.eye(length, k=1) + np.eye(length, k=-1))
    rows = np.arange(length)
    spread = np.zeros((length, length + 4))
    spread[rows, rows + 3] += near_coef
    spread[rows, rows + 1] -= near_coef
    spread[rows, rows + 4] += far_coef
    spread[rows, rows] -= far_coef
    return np.linalg.inv(matrix), spread


def split_table(table):
    table = np.asarray(table, np.float32)
    high = table.astype(jnp.bfloat16).astype(np.float32)
    return high, (table - high).astype(jnp.bfloat16).astype(np.float32)


def scaled_rows(table, diagonal):
    rows, width = table.shape
    reach = np.clip(np.asarray(diagonal)[:, None] + np.arange(-14, 15)[None, :], -1, width)
    padded = np.concatenate([np.zeros((rows, 1)), table, np.zeros((rows, 1))], axis=1)
    near, which = np.unique(
        np.round(np.take_along_axis(padded, reach + 1, axis=1), 12), axis=0, return_inverse=True
    )
    scales = np.exp2(np.arange(4096) / 4096.0)
    best = np.zeros(near.shape[0])
    for i, row in enumerate(near):
        tried = row[None, :] / scales[:, None]
        error = tried.astype(np.float32).astype(jnp.bfloat16).astype(np.float64) - tried
        best[i] = scales[np.argmin(np.sum(np.square(error * scales[:, None]), axis=1))]
    scale = best[which.reshape(-1)].astype(np.float32).astype(np.float64)
    values = (table / scale[:, None]).astype(np.float32).astype(jnp.bfloat16)
    return scale, values.astype(np.float32)


def block_tables(cells, groups):
    length = cells * groups
    inverse, spread = line_matrices(length)
    whole = -time_step * inverse @ spread[:, 2:-2]
    own = np.zeros((groups, cells, cells))
    beyond = np.zeros((groups, 4, cells))
    act = np.zeros((groups, 4, cells))
    for g in range(groups):
        s, e = g * cells, (g + 1) * cells
        own[g] = whole[s:e, s:e]
        if g > 0:
            beyond[g, 0] = whole[s - 1, s:e]
            beyond[g, 1] = whole[s - 2, s:e]
            act[g, 0, 0] = 1.0
            act[g, 1, 1:] = inverse[s + 1 : e, s] / inverse[s + 1, s]
        if g < groups - 1:
            beyond[g, 2] = whole[e, s:e]
            beyond[g, 3] = whole[e + 1, s:e]
            act[g, 2, cells - 1] = 1.0
            act[g, 3, : cells - 1] = inverse[s : e - 1, e - 1] / inverse[e - 2, e - 1]
    return own, beyond, act


def edge_scalars(beyond, cells):
    groups = beyond.shape[0]
    table = np.zeros((groups, 2 * cells + 4))
    table[:, :cells] = beyond[:, 1]
    table[:, cells : 2 * cells] = beyond[:, 3]
    for g in range(groups):
        if g > 0:
            table[g, 2 * cells] = beyond[g, 0, 1] / beyond[g, 1, 1]
            table[g, 2 * cells + 1] = beyond[g, 0, 0] - table[g, 2 * cells] * beyond[g, 1, 0]
        if g < groups - 1:
            table[g, 2 * cells + 2] = beyond[g, 2, cells - 2] / beyond[g, 3, cells - 2]
            table[g, 2 * cells + 3] = (
                beyond[g, 2, cells - 1] - table[g, 2 * cells + 2] * beyond[g, 3, cells - 1]
            )
    return table


def common(fields):
    rho, m1, m2, m3, energy = fields
    inv = 1.0 / rho
    pressure = 0.4 * (energy - 0.5 * inv * (m1 * m1 + m2 * m2 + m3 * m3))
    return inv, pressure, energy + pressure


def flux_from(fields, shared, direction):
    inv, pressure, total = shared
    velocity = fields[1 + direction] * inv
    out = [fields[1 + direction]]
    for component in range(3):
        term = fields[1 + component] * velocity
        out.append(term + pressure if component == direction else term)
    out.append(total * velocity)
    return out


def load_fields(rho, mom, ene, idx):
    return [rho[idx], mom[(0,) + idx], mom[(1,) + idx], mom[(2,) + idx], ene[idx]]


def split(value):
    high = value.astype(jnp.bfloat16)
    return high, (value - high.astype(jnp.float32)).astype(jnp.bfloat16)


def edge_kernel(place, cx, cy, weights, rho, mom, ene, xlo, xhi, ylo, yhi, ysum, *, cells, tile, last):
    step = pl.program_id(0)
    px, py = place[0], place[1]
    zs = rho.shape[2] // 128

    @pl.when(step == 0)
    def _():
        xlo[...] = jnp.zeros_like(xlo)
        xhi[...] = jnp.zeros_like(xhi)

    def piece(n, _):
        zc = pl.ds(pl.multiple_of(n * 128, 128), 128)
        for yy in range(0, cells, 16):
            ys = pl.ds(yy, 16)
            low = [xlo[f, 1, ys, zc] for f in range(5)]
            high = [xhi[f, 1, ys, zc] for f in range(5)]
            for x in range(tile):
                fields = load_fields(rho, mom, ene, (x, ys, zc))
                shared = common(fields)
                flux = flux_from(fields, shared, 0)
                cl = cx[px, step * tile + x]
                ch = cx[px, cells + step * tile + x]
                for f in range(5):
                    low[f] += cl * flux[f]
                    high[f] += ch * flux[f]
                if x == 0:
                    first = flux

                    @pl.when(step == 0)
                    def _():
                        for f in range(5):
                            xlo[f, 0, ys, zc] = cx[px, 2 * cells + 1] * first[f]

                if x == tile - 1:
                    end = flux

                    @pl.when(step == last)
                    def _():
                        for f in range(5):
                            xhi[f, 0, ys, zc] = cx[px, 2 * cells + 3] * end[f]

                side = flux_from(fields, shared, 1)
                row = pl.ds(x, 1)
                for f in range(5):
                    for d, out in ((0, ylo), (1, yhi)):
                        part = side[f] * weights[0, d, ys]
                        part = part[:8] + part[8:]
                        if yy > 0:
                            part += ysum[f, d, x]
                        if yy + 16 < cells:
                            ysum[f, d, x] = part
                        else:
                            total = jnp.sum(part, axis=0, keepdims=True)
                            out[f, 1, row, zc] = total
                            if d == 0:
                                out[f, 0, row, zc] += cy[py, 2 * cells] * total
                            else:
                                out[f, 0, row, zc] = (
                                    cy[py, 2 * cells + 2] * total + cy[py, 2 * cells + 3] * side[f][15:]
                                )
                    if yy == 0:
                        ylo[f, 0, row, zc] = cy[py, 2 * cells + 1] * side[f][:1]
            for f in range(5):
                xlo[f, 1, ys, zc] = low[f]
                xhi[f, 1, ys, zc] = high[f]

            @pl.when(step == last)
            def _():
                for f in range(5):
                    xlo[f, 0, ys, zc] += cx[px, 2 * cells] * low[f]
                    xhi[f, 0, ys, zc] += cx[px, 2 * cells + 2] * high[f]

        return 0

    lax.fori_loop(0, zs, piece, 0)


def lines_kernel(
    place, mx, my, mz, wz, sx, sy, sz, hg, rho, mom, ene, out,
    f_buf, g_buf, h_buf, acc, mx_buf, my_buf, mz_buf, *, cells, tile, steps
):
    step = pl.program_id(0)
    width = rho.shape[2]
    zs = width // 128
    rows = tile * cells
    bf16 = jnp.bfloat16
    dot = functools.partial(jnp.dot, preferred_element_type=jnp.float32)
    chunks = [(z * 128, (z + 1) * 128) for z in range(zs)]

    @pl.when(step == 0)
    def _():
        for buf, table in ((mx_buf, mx[0]), (my_buf, my[0])):
            buf[:, :rows] = table.astype(bf16)
            buf[:, rows:] = table.astype(bf16)
        mz_buf[...] = mz[...].astype(bf16)

    @pl.when(step < steps)
    def _():
        def piece(n, _):
            x = (n // (2 * zs)) * 2
            yy = pl.multiple_of((n // zs) % 2 * 16, 16)
            zc = pl.multiple_of((n % zs) * 128, 128)
            z_hi, z_lo = pl.ds(zc, 128), pl.ds(width + zc, 128)
            fields = load_fields(rho, mom, ene, (pl.ds(x, 2), pl.ds(yy, 16), z_hi))
            shared = common(fields)
            for f, value in enumerate(flux_from(fields, shared, 0)):
                for j in range(2):
                    hi, lo = split(value[:, 8 * j : 8 * j + 8].reshape(16, 128))
                    at = pl.multiple_of((step * tile + x) * 8, 16)
                    f_buf[yy // 8 + j, f, pl.ds(at, 16), z_hi] = hi
                    f_buf[yy // 8 + j, f, pl.ds(cells * 8 + at, 16), z_hi] = lo
            for f, value in enumerate(flux_from(fields, shared, 1)):
                for j in range(2):
                    hi, lo = split(value[j])
                    at = pl.multiple_of((x + j) * cells + yy, 16)
                    g_buf[f, pl.ds(at, 16), z_hi] = hi
                    g_buf[f, pl.ds(rows + at, 16), z_hi] = lo
            for f, value in enumerate(flux_from(fields, shared, 2)):
                for j in range(2):
                    hi, lo = split(value[j])
                    at = pl.multiple_of((x + j) * cells + yy, 16)
                    h_buf[f, pl.ds(at, 16), z_hi] = hi
                    h_buf[f, pl.ds(at, 16), z_lo] = lo
            return 0

        lax.fori_loop(0, (tile // 2) * 2 * zs, piece, 0)
        half = width // 2
        for f in range(5):
            base = rho if f == 0 else ene if f == 4 else mom.at[f - 1]
            y_part = dot(my_buf[...], g_buf[f])
            g_hi, g_lo = split(hg[f])
            g_hi, g_lo = g_hi.astype(jnp.float32), g_lo.astype(jnp.float32)
            ghost = jnp.concatenate([g_hi, g_lo, g_hi], axis=0).astype(bf16)
            for k in range(2):
                low = 0 if k == 0 else half - 128
                high = half + 128 if k == 0 else width
                left = jnp.concatenate([h_buf[f, :, low:high], h_buf[f, :, width + low : width + high]], axis=1)
                weight = mz_buf[low:high, k * half : (k + 1) * half]
                z_part = dot(left, jnp.concatenate([weight, weight], axis=0))
                edge = slice(0, 128) if k == 0 else slice(width - 128, width)
                ends = lax.dot_general(
                    ghost, wz[:, edge].astype(bf16), (((0,), (0,)), ((), ())),
                    preferred_element_type=jnp.float32,
                )
                for a, b in chunks[k * zs // 2 : (k + 1) * zs // 2]:
                    got = z_part[:, a - k * half : b - k * half]
                    if a == edge.start:
                        got = got + ends
                    got = got * sz[:, a:b] + y_part[:, a:b] * sy[0]
                    acc[f, pl.ds(step * tile, tile), :, a:b] = base[:, :, a:b] + got.reshape(tile, cells, 128)

    @pl.when(step >= steps)
    def _():
        j = step - steps
        at = pl.multiple_of(j * 8, 8)
        for f in range(5):
            got = dot(mx_buf[...], f_buf[j, f])
            for a, b in chunks:
                part = (got[:, a:b] * sx[0]).reshape(cells, 8, 128)
                out[f, :, :, a:b] = acc[f, :, pl.ds(at, 8), a:b] + part


def join_kernel(place, ax, ay, acc, xlo, xhi, ylo, yhi, out, *, cells, tile):
    step = pl.program_id(0)
    px = place[0]
    zs = acc.shape[3] // 128

    def piece(n, _):
        zc = pl.ds(pl.multiple_of(n * 128, 128), 128)
        for x in range(tile):
            i = step * tile + x
            at_low = jnp.where(i == 0, 0, 1)
            at_high = jnp.where(i == cells - 1, 0, 1)
            cl, ch = ax[px, i], ax[px, cells + i]
            for f in range(5):
                y_low, y_high = ylo[f, 1, x : x + 1, zc], yhi[f, 1, x : x + 1, zc]
                for yy in range(0, cells, 8):
                    ys = slice(yy, yy + 8)
                    term = acc[f, x, ys, zc] + cl * xlo[f, at_low, ys, zc] + ch * xhi[f, at_high, ys, zc]
                    term += ay[0, 1, ys] * y_low + ay[0, 3, ys] * y_high
                    if yy == 0:
                        term += ay[0, 0, ys] * ylo[f, 0, x : x + 1, zc]
                    if yy + 8 == cells:
                        term += ay[0, 2, ys] * yhi[f, 0, x : x + 1, zc]
                    out[f, x, ys, zc] = term
        return 0

    lax.fori_loop(0, zs, piece, 0)


def ghost_fluxes(coarse_rows, ghost_rows, time_index, groups_x, place_x, cells):
    slots = ghost_rows.shape[2]
    capacity = slots // groups_x
    block = coarse_rows.shape[1]
    rows = ghost_rows[0]
    weights = time_index[0].astype(jnp.float32) * 0.125
    mine = (rows // block == place_x).astype(jnp.int32)
    upper = (np.arange(slots)[:, None] <= np.arange(slots)[None, :]).astype(np.float32)
    rank = jnp.dot(mine.astype(jnp.float32), upper, precision=highest).astype(jnp.int32) - 1
    wanted = jnp.arange(capacity, dtype=jnp.int32)
    pick = (mine[:, None, :] > 0) & (rank[:, None, :] == wanted[None, :, None])
    local_rows = jnp.sum(jnp.where(pick, (rows - place_x * block)[:, None, :], 0), axis=2).reshape(-1)
    level = jnp.sum(jnp.where(pick, weights[:, None, :], 0.0), axis=2).reshape(-1, 1)
    onehot = (local_rows[:, None] == jnp.arange(block)[None, :]).astype(jnp.float32)
    old = jnp.dot(onehot, coarse_rows[0, :, 0, :], precision=highest)
    new = jnp.dot(onehot, coarse_rows[1, :, 0, :], precision=highest)
    sent = ((1.0 - level) * old + level * new).reshape(groups_x, capacity, -1)
    every = lax.all_gather(sent, "gx")
    got = lax.dynamic_index_in_dim(every, place_x, 1, keepdims=False).reshape(slots, -1)
    owner = lax.dynamic_index_in_dim(rows, place_x, 0, keepdims=False) // block
    earlier = np.arange(slots)[None, :] < np.arange(slots)[:, None]
    nth = jnp.sum(((owner[:, None] == owner[None, :]) & earlier).astype(jnp.int32), axis=1)
    back = ((owner * capacity + nth)[:, None] == jnp.arange(slots)[None, :]).astype(jnp.float32)
    ghosts = jnp.dot(back, got, precision=highest).reshape(4, cells, 5, cells)
    fields = [ghosts[:, :, f] for f in range(5)]
    flux = jnp.stack(flux_from(fields, common(fields), 2)).reshape(5, 4, cells * cells)
    return jnp.pad(flux, ((0, 0), (0, 4), (0, 0)))


def local(density, momentum, energy, coarse_rows, ghost_rows, time_index):
    cells, _, cells_z = density.shape
    groups_x, groups_y = lax.axis_size("gx"), lax.axis_size("gy")
    place_x, place_y = lax.axis_index("gx"), lax.axis_index("gy")
    place = jnp.stack([place_x, place_y]).astype(jnp.int32)
    tile = 8
    steps = cells // tile
    f32 = jnp.float32

    own_x, beyond_x, act_x = block_tables(cells, groups_x)
    own_y, beyond_y, act_y = block_tables(cells, groups_y)
    inverse_z, spread_z = line_matrices(cells_z)
    whole_z = -time_step * inverse_z @ spread_z
    at_x = np.tile(np.arange(cells), groups_x)
    at_y = np.tile(np.arange(cells), groups_y)
    scale_x, values_x = scaled_rows(own_x.reshape(-1, cells), at_x)
    scale_y, values_y = scaled_rows(own_y.reshape(-1, cells), at_y)
    scale_z, values_z = scaled_rows(whole_z[:, 2:-2], np.arange(cells_z))
    lanes = np.ones((1, 128), np.float32)
    mx = np.stack([np.kron(m, np.eye(8)) for m in values_x.reshape(own_x.shape)]).astype(np.float32)
    my = np.stack([np.kron(np.eye(tile), m) for m in values_y.reshape(own_y.shape)]).astype(np.float32)
    mz = np.ascontiguousarray(values_z.T)
    sx = np.stack([np.repeat(v, 8)[:, None] * lanes for v in scale_x.reshape(groups_x, cells)])
    sy = np.stack([np.tile(v, tile)[:, None] * lanes for v in scale_y.reshape(groups_y, cells)])
    sx, sy, sz = sx.astype(np.float32), sy.astype(np.float32), scale_z[None, :].astype(np.float32)
    ends = np.zeros((8, cells_z), np.float32)
    ends[:4] = (whole_z[:, [0, 1, cells_z + 2, cells_z + 3]] / scale_z[:, None]).T
    ends_hi, ends_lo = split_table(ends)
    wz = np.concatenate([ends_hi, ends_hi, ends_lo])
    cy = edge_scalars(beyond_y, cells).astype(np.float32)
    weights = np.broadcast_to(beyond_y[:, 1::2, :, None], (groups_y, 2, cells, 128)).astype(np.float32)
    cx = edge_scalars(beyond_x, cells).astype(np.float32)
    ax = np.concatenate([act_x[:, 0] + act_x[:, 1], act_x[:, 2] + act_x[:, 3]], axis=1).astype(np.float32)
    ay = np.broadcast_to(act_y[..., None], act_y.shape + (128,)).astype(np.float32)

    hg = ghost_fluxes(coarse_rows, ghost_rows, time_index, groups_x, place_x, cells)

    smem = pl.BlockSpec(memory_space=pltpu.SMEM)
    xtile3 = pl.BlockSpec((tile, cells, cells_z), lambda i, p: (i, 0, 0))
    xtile4 = pl.BlockSpec((3, tile, cells, cells_z), lambda i, p: (0, i, 0, 0))
    xtile5 = pl.BlockSpec((5, tile, cells, cells_z), lambda i, p: (0, i, 0, 0))
    xplane = pl.BlockSpec((5, 2, cells, cells_z), lambda i, p: (0, 0, 0, 0))
    yplane = pl.BlockSpec((5, 2, tile, cells_z), lambda i, p: (0, 0, i, 0))
    params = pltpu.CompilerParams(vmem_limit_bytes=vmem_bytes, dimension_semantics=("arbitrary",))
    planes = jax.ShapeDtypeStruct((5, 2, cells, cells_z), f32)
    whole = jax.ShapeDtypeStruct((5, cells, cells, cells_z), f32)

    def fixed(table, which=None):
        dims = table.shape[1:]
        if which is None:
            return pl.BlockSpec(table.shape, lambda i, p: (0,) * table.ndim)
        return pl.BlockSpec((1,) + dims, lambda i, p: (p[which],) + (0,) * len(dims))

    def call(kernel, in_specs, out_shape, out_specs, scratch, cost, grid=steps, **more):
        return pl.pallas_call(
            kernel,
            grid_spec=pltpu.PrefetchScalarGridSpec(
                num_scalar_prefetch=1, grid=(grid,), in_specs=in_specs, out_specs=out_specs,
                scratch_shapes=scratch,
            ),
            out_shape=out_shape,
            compiler_params=params,
            cost_estimate=pl.CostEstimate(flops=cost[0], bytes_accessed=cost[1], transcendentals=0),
            **more,
        )

    size = 4 * 5 * cells * cells * cells_z
    rows = tile * cells
    bf16 = jnp.bfloat16
    xlo, xhi, ylo, yhi = call(
        functools.partial(edge_kernel, cells=cells, tile=tile, last=steps - 1),
        [smem, smem, fixed(weights, 1), xtile3, xtile4, xtile3],
        [planes] * 4,
        [xplane, xplane, yplane, yplane],
        [pltpu.VMEM((5, 2, tile, 8, 128), f32)],
        (size * 20, size),
        name="edges",
    )(place, cx, cy, weights, density, momentum, energy)

    def shift(array, axis, by):
        peers = lax.axis_size(axis)
        return lax.ppermute(
            array, axis, [(i, i + by) for i in range(peers) if 0 <= i + by < peers]
        )

    in_xlo = shift(xhi, "gx", 1)
    in_xhi = shift(xlo, "gx", -1)
    in_ylo = shift(yhi, "gy", 1)
    in_yhi = shift(ylo, "gy", -1)

    top = steps - 1
    acc = call(
        functools.partial(lines_kernel, cells=cells, tile=tile, steps=steps),
        [
            fixed(mx, 0), fixed(my, 1), fixed(mz), fixed(wz), fixed(sx, 0), fixed(sy, 1), fixed(sz),
            pl.BlockSpec((5, 8, rows), lambda i, p: (0, 0, jnp.minimum(i, top))),
            pl.BlockSpec((tile, cells, cells_z), lambda i, p: (jnp.minimum(i, top), 0, 0)),
            pl.BlockSpec((3, tile, cells, cells_z), lambda i, p: (0, jnp.minimum(i, top), 0, 0)),
            pl.BlockSpec((tile, cells, cells_z), lambda i, p: (jnp.minimum(i, top), 0, 0)),
        ],
        whole,
        pl.BlockSpec((5, cells, 8, cells_z), lambda i, p: (0, 0, jnp.maximum(i - steps, 0), 0)),
        [
            pltpu.VMEM((cells // 8, 5, 2 * cells * 8, cells_z), bf16),
            pltpu.VMEM((5, 2 * rows, cells_z), bf16),
            pltpu.VMEM((5, rows, 2 * cells_z), bf16),
            pltpu.VMEM((5, cells, cells, cells_z), f32),
            pltpu.VMEM((cells * 8, 2 * cells * 8), bf16),
            pltpu.VMEM((rows, 2 * rows), bf16),
            pltpu.VMEM((cells_z, cells_z), bf16),
        ],
        (size * 1200, 2 * size),
        grid=2 * steps,
        name="lines",
    )(place, mx, my, mz, wz, sx, sy, sz, hg, density, momentum, energy)
    return call(
        functools.partial(join_kernel, cells=cells, tile=tile),
        [smem, fixed(ay, 1), xtile5, xplane, xplane, yplane, yplane],
        whole,
        xtile5,
        [],
        (size * 4, 2 * size),
        name="join",
    )(place, ax, ay, acc, in_xlo, in_xhi, in_ylo, in_yhi)


def solution(mesh):
    return jax.shard_map(
        local,
        mesh=mesh,
        in_specs=(
            P("gx", "gy", None),
            P(None, "gx", "gy", None),
            P("gx", "gy", None),
            P(None, "gx", "gy", None),
            P("gy", None, None),
            P("gy", None, None),
        ),
        out_specs=P(None, "gx", "gy", None),
        check_vma=False,
    )
```

```python
import functools

import jax
import jax.numpy as jnp
import numpy as np
from jax import lax
from jax.experimental import pallas as pl
from jax.experimental.pallas import tpu as pltpu
from jax.sharding import PartitionSpec as P

beta_coef = 1.0 / 3.0
near_coef = 7.0 / 9.0
far_coef = 1.0 / 36.0
time_step = 0.4
highest = lax.Precision.HIGHEST
vmem_bytes = 63 * 1024 * 1024


def line_matrices(length):
    matrix = np.eye(length) + beta_coef * (np.eye(length, k=1) + np.eye(length, k=-1))
    rows = np.arange(length)
    spread = np.zeros((length, length + 4))
    spread[rows, rows + 3] += near_coef
    spread[rows, rows + 1] -= near_coef
    spread[rows, rows + 4] += far_coef
    spread[rows, rows] -= far_coef
    return np.linalg.inv(matrix), spread


def scaled_rows(table, diagonal):
    rows, width = table.shape
    reach = np.clip(np.asarray(diagonal)[:, None] + np.arange(-14, 15)[None, :], -1, width)
    padded = np.concatenate([np.zeros((rows, 1)), table, np.zeros((rows, 1))], axis=1)
    near, which = np.unique(
        np.round(np.take_along_axis(padded, reach + 1, axis=1), 12), axis=0, return_inverse=True
    )
    scales = np.exp2(np.arange(4096) / 4096.0)
    best = np.zeros(near.shape[0])
    for i, row in enumerate(near):
        tried = row[None, :] / scales[:, None]
        error = tried.astype(np.float32).astype(jnp.bfloat16).astype(np.float64) - tried
        best[i] = scales[np.argmin(np.sum(np.square(error * scales[:, None]), axis=1))]
    scale = best[which.reshape(-1)].astype(np.float32).astype(np.float64)
    values = (table / scale[:, None]).astype(np.float32).astype(jnp.bfloat16)
    return scale, values.astype(np.float32)


def block_tables(cells, groups):
    length = cells * groups
    inverse, spread = line_matrices(length)
    whole = -time_step * inverse @ spread[:, 2:-2]
    own = np.zeros((groups, cells, cells))
    beyond = np.zeros((groups, 4, cells))
    act = np.zeros((groups, 4, cells))
    for g in range(groups):
        s, e = g * cells, (g + 1) * cells
        own[g] = whole[s:e, s:e]
        if g > 0:
            beyond[g, 0] = whole[s - 1, s:e]
            beyond[g, 1] = whole[s - 2, s:e]
            act[g, 0, 0] = 1.0
            act[g, 1, 1:] = inverse[s + 1 : e, s] / inverse[s + 1, s]
        if g < groups - 1:
            beyond[g, 2] = whole[e, s:e]
            beyond[g, 3] = whole[e + 1, s:e]
            act[g, 2, cells - 1] = 1.0
            act[g, 3, : cells - 1] = inverse[s : e - 1, e - 1] / inverse[e - 2, e - 1]
    return own, beyond, act


def edge_scalars(beyond, cells):
    groups = beyond.shape[0]
    table = np.zeros((groups, 2 * cells + 4))
    table[:, :cells] = beyond[:, 1]
    table[:, cells : 2 * cells] = beyond[:, 3]
    for g in range(groups):
        if g > 0:
            table[g, 2 * cells] = beyond[g, 0, 1] / beyond[g, 1, 1]
            table[g, 2 * cells + 1] = beyond[g, 0, 0] - table[g, 2 * cells] * beyond[g, 1, 0]
        if g < groups - 1:
            table[g, 2 * cells + 2] = beyond[g, 2, cells - 2] / beyond[g, 3, cells - 2]
            table[g, 2 * cells + 3] = (
                beyond[g, 2, cells - 1] - table[g, 2 * cells + 2] * beyond[g, 3, cells - 1]
            )
    return table


def common(fields):
    rho, m1, m2, m3, energy = fields
    inv = 1.0 / rho
    pressure = 0.4 * (energy - 0.5 * inv * (m1 * m1 + m2 * m2 + m3 * m3))
    return inv, pressure, energy + pressure


def flux_from(fields, shared, direction):
    inv, pressure, total = shared
    velocity = fields[1 + direction] * inv
    out = [fields[1 + direction]]
    for component in range(3):
        term = fields[1 + component] * velocity
        out.append(term + pressure if component == direction else term)
    out.append(total * velocity)
    return out


def load_fields(rho, mom, ene, idx):
    return [rho[idx], mom[(0,) + idx], mom[(1,) + idx], mom[(2,) + idx], ene[idx]]


def split(value):
    high = value.astype(jnp.bfloat16)
    return high, (value - high.astype(jnp.float32)).astype(jnp.bfloat16)


def edge_kernel(place, cx, cy, weights, _, rho, mom, ene, xlo, xhi, ylo, yhi, ysum, *, cells, tile, last):
    step = pl.program_id(0)
    px, py = place[0], place[1]
    zs = rho.shape[2] // 128

    @pl.when(step == 0)
    def _():
        xlo[...] = jnp.zeros_like(xlo)
        xhi[...] = jnp.zeros_like(xhi)

    def piece(n, _):
        zc = pl.ds(pl.multiple_of(n * 128, 128), 128)
        for yy in range(0, cells, 16):
            ys = pl.ds(yy, 16)
            low = [xlo[f, 1, ys, zc] for f in range(5)]
            high = [xhi[f, 1, ys, zc] for f in range(5)]
            for x in range(tile):
                fields = load_fields(rho, mom, ene, (x, ys, zc))
                shared = common(fields)
                flux = flux_from(fields, shared, 0)
                cl = cx[px, step * tile + x]
                ch = cx[px, cells + step * tile + x]
                for f in range(5):
                    low[f] += cl * flux[f]
                    high[f] += ch * flux[f]
                if x == 0:
                    first = flux

                    @pl.when(step == 0)
                    def _():
                        for f in range(5):
                            xlo[f, 0, ys, zc] = cx[px, 2 * cells + 1] * first[f]

                if x == tile - 1:
                    end = flux

                    @pl.when(step == last)
                    def _():
                        for f in range(5):
                            xhi[f, 0, ys, zc] = cx[px, 2 * cells + 3] * end[f]

                side = flux_from(fields, shared, 1)
                row = pl.ds(x, 1)
                for f in range(5):
                    for d, out in ((0, ylo), (1, yhi)):
                        part = side[f] * weights[0, d, ys]
                        part = part[:8] + part[8:]
                        if yy > 0:
                            part += ysum[f, d, x]
                        if yy + 16 < cells:
                            ysum[f, d, x] = part
                        else:
                            total = jnp.sum(part, axis=0, keepdims=True)
                            out[f, 1, row, zc] = total
                            if d == 0:
                                out[f, 0, row, zc] += cy[py, 2 * cells] * total
                            else:
                                out[f, 0, row, zc] = (
                                    cy[py, 2 * cells + 2] * total + cy[py, 2 * cells + 3] * side[f][15:]
                                )
                    if yy == 0:
                        ylo[f, 0, row, zc] = cy[py, 2 * cells + 1] * side[f][:1]
            for f in range(5):
                xlo[f, 1, ys, zc] = low[f]
                xhi[f, 1, ys, zc] = high[f]

            @pl.when(step == last)
            def _():
                for f in range(5):
                    xlo[f, 0, ys, zc] += cx[px, 2 * cells] * low[f]
                    xhi[f, 0, ys, zc] += cx[px, 2 * cells + 2] * high[f]

        return 0

    lax.fori_loop(0, zs, piece, 0)


def lines_kernel(
    place, mx, my, mz, wz, sx, sy, sz, hg, rho, mom, ene, out,
    f_buf, g_buf, h_buf, acc, mx_buf, my_buf, mz_buf, *, cells, tile, steps
):
    step = pl.program_id(0)
    width = rho.shape[2]
    zs = width // 128
    rows = tile * cells
    bf16 = jnp.bfloat16
    dot = functools.partial(jnp.dot, preferred_element_type=jnp.float32)
    chunks = [(z * 128, (z + 1) * 128) for z in range(zs)]

    @pl.when(step == 0)
    def _():
        for buf, table in ((mx_buf, mx[0]), (my_buf, my[0])):
            buf[:, :rows] = table.astype(bf16)
            buf[:, rows:] = table.astype(bf16)
        mz_buf[...] = mz[...].astype(bf16)

    @pl.when(step < steps)
    def _():
        def piece(n, _):
            x = (n // (2 * zs)) * 2
            yy = pl.multiple_of((n // zs) % 2 * 16, 16)
            zc = pl.multiple_of((n % zs) * 128, 128)
            z_hi, z_lo = pl.ds(zc, 128), pl.ds(width + zc, 128)
            fields = load_fields(rho, mom, ene, (pl.ds(x, 2), pl.ds(yy, 16), z_hi))
            shared = common(fields)
            for f, value in enumerate(flux_from(fields, shared, 0)):
                for j in range(2):
                    hi, lo = split(value[:, 8 * j : 8 * j + 8].reshape(16, 128))
                    at = pl.multiple_of((step * tile + x) * 8, 16)
                    f_buf[yy // 8 + j, f, pl.ds(at, 16), z_hi] = hi
                    f_buf[yy // 8 + j, f, pl.ds(cells * 8 + at, 16), z_hi] = lo
            for f, value in enumerate(flux_from(fields, shared, 1)):
                for j in range(2):
                    hi, lo = split(value[j])
                    at = pl.multiple_of((x + j) * cells + yy, 16)
                    g_buf[f, pl.ds(at, 16), z_hi] = hi
                    g_buf[f, pl.ds(rows + at, 16), z_hi] = lo
            for f, value in enumerate(flux_from(fields, shared, 2)):
                for j in range(2):
                    hi, lo = split(value[j])
                    at = pl.multiple_of((x + j) * cells + yy, 16)
                    h_buf[f, pl.ds(at, 16), z_hi] = hi
                    h_buf[f, pl.ds(at, 16), z_lo] = lo
            return 0

        lax.fori_loop(0, (tile // 2) * 2 * zs, piece, 0)
        half = width // 2
        slots = hg.shape[2]
        own_slot = jnp.where(
            lax.broadcasted_iota(jnp.int32, (rows, slots), 1) % cells
            == lax.broadcasted_iota(jnp.int32, (rows, slots), 0) // cells + step * tile,
            1.0, 0.0,
        )
        for f in range(5):
            base = rho if f == 0 else ene if f == 4 else mom.at[f - 1]
            y_part = dot(my_buf[...], g_buf[f])
            g_hi, g_lo = split(jnp.concatenate([hg[f]] * tile, axis=0) * own_slot)
            ghost = jnp.concatenate([g_hi, g_lo], axis=1)
            for k in range(2):
                low = 0 if k == 0 else half - 128
                high = half + 128 if k == 0 else width
                left = jnp.concatenate([h_buf[f, :, low:high], h_buf[f, :, width + low : width + high]], axis=1)
                weight = mz_buf[low:high, k * half : (k + 1) * half]
                z_part = dot(left, jnp.concatenate([weight, weight], axis=0))
                edge = slice(0, 128) if k == 0 else slice(width - 128, width)
                ends = dot(ghost, wz[:, edge].astype(bf16))
                for a, b in chunks[k * zs // 2 : (k + 1) * zs // 2]:
                    got = z_part[:, a - k * half : b - k * half]
                    if a == edge.start:
                        got = got + ends
                    got = got * sz[:, a:b] + y_part[:, a:b] * sy[0]
                    acc[f, pl.ds(step * tile, tile), :, a:b] = base[:, :, a:b] + got.reshape(tile, cells, 128)

    @pl.when(step >= steps)
    def _():
        j = step - steps
        at = pl.multiple_of(j * 8, 8)
        for f in range(5):
            got = dot(mx_buf[...], f_buf[j, f])
            for a, b in chunks:
                part = (got[:, a:b] * sx[0]).reshape(cells, 8, 128)
                out[f, :, :, a:b] = acc[f, :, pl.ds(at, 8), a:b] + part


def join_kernel(place, ax, ay, acc, xlo, xhi, ylo, yhi, out, *, cells, tile, last):
    step = pl.program_id(0)
    px = place[0]
    zs = acc.shape[3] // 128

    def piece(n, _):
        zc = pl.ds(pl.multiple_of(n * 128, 128), 128)
        weights = [(ax[px, step * tile + x], ax[px, cells + step * tile + x]) for x in range(tile)]
        for yy in range(0, cells, 8):
            ys = slice(yy, yy + 8)
            a_low, a_high = ay[0, 1, ys], ay[0, 3, ys]
            for f in range(5):
                x_low, x_high = xlo[f, 1, ys, zc], xhi[f, 1, ys, zc]
                for x in range(tile):
                    row = slice(x, x + 1)
                    term = acc[f, x, ys, zc] + weights[x][0] * x_low + weights[x][1] * x_high
                    term += a_low * ylo[f, 1, row, zc] + a_high * yhi[f, 1, row, zc]
                    if yy == 0:
                        term += ay[0, 0, ys] * ylo[f, 0, row, zc]
                    if yy + 8 == cells:
                        term += ay[0, 2, ys] * yhi[f, 0, row, zc]
                    out[f, x, ys, zc] = term
        return 0

    lax.fori_loop(0, zs, piece, 0)

    @pl.when(step == 0)
    def _():
        for f in range(5):
            out[f, 0] += xlo[f, 0]

    @pl.when(step == last)
    def _():
        for f in range(5):
            out[f, tile - 1] += xhi[f, 0]


def ghost_kernel(rows_ref, time_ref, coarse, out, sent, got, send_sem, recv_sem, *, groups, cells):
    me = lax.axis_index("gx")
    slots = rows_ref.shape[1]
    block = coarse.shape[2]
    cap = slots // groups
    f32 = jnp.float32
    highest_dot = functools.partial(
        lax.dot_general, precision=highest, preferred_element_type=f32
    )
    barrier = pltpu.get_barrier_semaphore()
    for off in range(1, groups):
        pl.semaphore_signal(
            barrier, inc=1, device_id={"gx": lax.rem(me + off, groups)}, device_id_type=pl.DeviceIdType.MESH
        )

    rows = rows_ref[...]
    first = me * block
    mine = jnp.where((rows >= first) & (rows < first + block), 1.0, 0.0)
    upper = jnp.where(
        lax.broadcasted_iota(jnp.int32, (slots, slots), 0) <= lax.broadcasted_iota(jnp.int32, (slots, slots), 1),
        1.0, 0.0,
    )
    rank = jnp.where(mine > 0.5, jnp.dot(mine, upper, preferred_element_type=f32) - 1.0, -1.0)
    wanted = lax.broadcasted_iota(jnp.int32, (cap, slots), 0).astype(f32)
    local_rows = (rows - first).astype(f32)
    level = time_ref[...].astype(f32) * 0.125
    picked, levels = [], []
    for a in range(groups):
        pick = rank[a : a + 1] == wanted
        picked.append(jnp.sum(jnp.where(pick, local_rows[a : a + 1], 0.0), axis=1, keepdims=True))
        levels.append(jnp.sum(jnp.where(pick, level[a : a + 1], 0.0), axis=1, keepdims=True))
    picked = jnp.concatenate(picked, axis=0)
    levels = jnp.concatenate(levels, axis=0)
    onehot = jnp.where(
        picked == lax.broadcasted_iota(jnp.int32, (slots, block), 1).astype(f32), 1.0, 0.0
    )
    contract = (((1,), (1,)), ((), ()))
    old = highest_dot(onehot, coarse[0], contract)
    new = highest_dot(onehot, coarse[1], contract)
    sent[...] = (1.0 - levels) * old + levels * new

    pl.semaphore_wait(barrier, groups - 1)
    here = pl.ds(pl.multiple_of(me * cap, cap), cap)
    copies = []
    for off in range(1, groups):
        target = lax.rem(me + off, groups)
        copy = pltpu.make_async_remote_copy(
            src_ref=sent.at[pl.ds(pl.multiple_of(target * cap, cap), cap)],
            dst_ref=got.at[here],
            send_sem=send_sem.at[off],
            recv_sem=recv_sem.at[off],
            device_id={"gx": target},
            device_id_type=pl.DeviceIdType.MESH,
        )
        copy.start()
        copies.append(copy)
    got[here] = sent[here]
    own = rows_ref[pl.ds(me, 1)]
    source = lax.broadcasted_iota(jnp.int32, (groups, slots), 0) * block
    match = jnp.where((own >= source) & (own < source + block), 1.0, 0.0)
    nth = jnp.dot(match, upper, preferred_element_type=f32) - 1.0
    base = lax.broadcasted_iota(jnp.int32, (groups, slots), 0).astype(f32) * cap
    index = jnp.sum(match * (nth + base), axis=0, keepdims=True)
    back = jnp.where(lax.broadcasted_iota(jnp.int32, (slots, slots), 0).astype(f32) == index, 1.0, 0.0)
    for copy in copies:
        copy.wait()
    ghosts = highest_dot(got[...], back, (((0,), (0,)), ((), ())))
    fields = [ghosts[f * cells : (f + 1) * cells] for f in range(5)]
    for f, value in enumerate(flux_from(fields, common(fields), 2)):
        out[f] = value


def ghost_fluxes(coarse_rows, ghost_rows, time_index, cells):
    groups = lax.axis_size("gx")
    slots = ghost_rows.shape[2]
    width = coarse_rows.shape[3]
    vmem = pl.BlockSpec(memory_space=pltpu.VMEM)
    return pl.pallas_call(
        functools.partial(ghost_kernel, groups=groups, cells=cells),
        out_shape=jax.ShapeDtypeStruct((5, cells, slots), jnp.float32),
        in_specs=[vmem] * 3,
        out_specs=vmem,
        scratch_shapes=[
            pltpu.VMEM((slots, width), jnp.float32),
            pltpu.VMEM((slots, width), jnp.float32),
            pltpu.SemaphoreType.DMA((groups,)),
            pltpu.SemaphoreType.DMA((groups,)),
        ],
        compiler_params=pltpu.CompilerParams(
            collective_id=0, has_side_effects=True, vmem_limit_bytes=vmem_bytes
        ),
        cost_estimate=pl.CostEstimate(flops=1 << 24, bytes_accessed=1 << 20, transcendentals=0),
        name="ghosts",
    )(ghost_rows[0], time_index[0], coarse_rows[:, :, 0, :].transpose(0, 2, 1))


def local(density, momentum, energy, coarse_rows, ghost_rows, time_index):
    cells, _, cells_z = density.shape
    groups_x, groups_y = lax.axis_size("gx"), lax.axis_size("gy")
    place_x, place_y = lax.axis_index("gx"), lax.axis_index("gy")
    place = jnp.stack([place_x, place_y]).astype(jnp.int32)
    tile = 8
    steps = cells // tile
    f32 = jnp.float32

    own_x, beyond_x, act_x = block_tables(cells, groups_x)
    own_y, beyond_y, act_y = block_tables(cells, groups_y)
    inverse_z, spread_z = line_matrices(cells_z)
    whole_z = -time_step * inverse_z @ spread_z
    at_x = np.tile(np.arange(cells), groups_x)
    at_y = np.tile(np.arange(cells), groups_y)
    scale_x, values_x = scaled_rows(own_x.reshape(-1, cells), at_x)
    scale_y, values_y = scaled_rows(own_y.reshape(-1, cells), at_y)
    scale_z, values_z = scaled_rows(whole_z, np.arange(cells_z) + 2)
    lanes = np.ones((1, 128), np.float32)
    mx = np.stack([np.kron(m, np.eye(8)) for m in values_x.reshape(own_x.shape)]).astype(np.float32)
    my = np.stack([np.kron(np.eye(tile), m) for m in values_y.reshape(own_y.shape)]).astype(np.float32)
    mz = np.ascontiguousarray(values_z[:, 2:-2].T)
    sx = np.stack([np.repeat(v, 8)[:, None] * lanes for v in scale_x.reshape(groups_x, cells)])
    sy = np.stack([np.tile(v, tile)[:, None] * lanes for v in scale_y.reshape(groups_y, cells)])
    sx, sy, sz = sx.astype(np.float32), sy.astype(np.float32), scale_z[None, :].astype(np.float32)
    wz = np.tile(np.repeat(values_z[:, [0, 1, cells_z + 2, cells_z + 3]].T, cells, axis=0), (2, 1))
    cy = edge_scalars(beyond_y, cells).astype(np.float32)
    weights = np.broadcast_to(beyond_y[:, 1::2, :, None], (groups_y, 2, cells, 128)).astype(np.float32)
    cx = edge_scalars(beyond_x, cells).astype(np.float32)
    ax = np.concatenate([act_x[:, 1], act_x[:, 3]], axis=1).astype(np.float32)
    ay = np.broadcast_to(act_y[..., None], act_y.shape + (128,)).astype(np.float32)

    hg = ghost_fluxes(coarse_rows, ghost_rows, time_index, cells)

    smem = pl.BlockSpec(memory_space=pltpu.SMEM)
    xtile3 = pl.BlockSpec((tile, cells, cells_z), lambda i, p: (i, 0, 0))
    xtile4 = pl.BlockSpec((3, tile, cells, cells_z), lambda i, p: (0, i, 0, 0))
    xtile5 = pl.BlockSpec((5, tile, cells, cells_z), lambda i, p: (0, i, 0, 0))
    xplane = pl.BlockSpec((5, 2, cells, cells_z), lambda i, p: (0, 0, 0, 0))
    yplane = pl.BlockSpec((5, 2, tile, cells_z), lambda i, p: (0, 0, i, 0))
    params = pltpu.CompilerParams(vmem_limit_bytes=vmem_bytes, dimension_semantics=("arbitrary",))
    planes = jax.ShapeDtypeStruct((5, 2, cells, cells_z), f32)
    whole = jax.ShapeDtypeStruct((5, cells, cells, cells_z), f32)

    def fixed(table, which=None):
        dims = table.shape[1:]
        if which is None:
            return pl.BlockSpec(table.shape, lambda i, p: (0,) * table.ndim)
        return pl.BlockSpec((1,) + dims, lambda i, p: (p[which],) + (0,) * len(dims))

    def call(kernel, in_specs, out_shape, out_specs, scratch, cost, grid=steps, **more):
        return pl.pallas_call(
            kernel,
            grid_spec=pltpu.PrefetchScalarGridSpec(
                num_scalar_prefetch=1, grid=(grid,), in_specs=in_specs, out_specs=out_specs,
                scratch_shapes=scratch,
            ),
            out_shape=out_shape,
            compiler_params=params,
            cost_estimate=pl.CostEstimate(flops=cost[0], bytes_accessed=cost[1], transcendentals=0),
            **more,
        )

    size = 4 * 5 * cells * cells * cells_z
    rows = tile * cells
    bf16 = jnp.bfloat16
    xlo, xhi, ylo, yhi = call(
        functools.partial(edge_kernel, cells=cells, tile=tile, last=steps - 1),
        [smem, smem, fixed(weights, 1), pl.BlockSpec(memory_space=pl.ANY), xtile3, xtile4, xtile3],
        [planes] * 4,
        [xplane, xplane, yplane, yplane],
        [pltpu.VMEM((5, 2, tile, 8, 128), f32)],
        (size * 20, size),
        name="edges",
    )(place, cx, cy, weights, hg, density, momentum, energy)

    def shift(array, axis, by):
        peers = lax.axis_size(axis)
        return lax.ppermute(
            array, axis, [(i, i + by) for i in range(peers) if 0 <= i + by < peers]
        )

    in_xlo = shift(xhi, "gx", 1)
    in_xhi = shift(xlo, "gx", -1)
    in_ylo = shift(yhi, "gy", 1)
    in_yhi = shift(ylo, "gy", -1)

    top = steps - 1
    acc = call(
        functools.partial(lines_kernel, cells=cells, tile=tile, steps=steps),
        [
            fixed(mx, 0), fixed(my, 1), fixed(mz), fixed(wz), fixed(sx, 0), fixed(sy, 1), fixed(sz),
            fixed(hg),
            pl.BlockSpec((tile, cells, cells_z), lambda i, p: (jnp.minimum(i, top), 0, 0)),
            pl.BlockSpec((3, tile, cells, cells_z), lambda i, p: (0, jnp.minimum(i, top), 0, 0)),
            pl.BlockSpec((tile, cells, cells_z), lambda i, p: (jnp.minimum(i, top), 0, 0)),
        ],
        whole,
        pl.BlockSpec((5, cells, 8, cells_z), lambda i, p: (0, 0, jnp.maximum(i - steps, 0), 0)),
        [
            pltpu.VMEM((cells // 8, 5, 2 * cells * 8, cells_z), bf16),
            pltpu.VMEM((5, 2 * rows, cells_z), bf16),
            pltpu.VMEM((5, rows, 2 * cells_z), bf16),
            pltpu.VMEM((5, cells, cells, cells_z), f32),
            pltpu.VMEM((cells * 8, 2 * cells * 8), bf16),
            pltpu.VMEM((rows, 2 * rows), bf16),
            pltpu.VMEM((cells_z, cells_z), bf16),
        ],
        (size * 1200, 2 * size),
        grid=2 * steps,
        name="lines",
    )(place, mx, my, mz, wz, sx, sy, sz, hg, density, momentum, energy)
    return call(
        functools.partial(join_kernel, cells=cells, tile=tile, last=steps - 1),
        [smem, fixed(ay, 1), xtile5, xplane, xplane, yplane, yplane],
        whole,
        xtile5,
        [],
        (size * 4, 2 * size),
        name="join",
    )(place, ax, ay, acc, in_xlo, in_xhi, in_ylo, in_yhi)


def solution(mesh):
    return jax.shard_map(
        local,
        mesh=mesh,
        in_specs=(
            P("gx", "gy", None),
            P(None, "gx", "gy", None),
            P("gx", "gy", None),
            P(None, "gx", "gy", None),
            P("gy", None, None),
            P("gy", None, None),
        ),
        out_specs=P(None, "gx", "gy", None),
        check_vma=False,
    )
```

```python
import functools

import jax
import jax.numpy as jnp
import numpy as np
from jax import lax
from jax.experimental import pallas as pl
from jax.experimental.pallas import tpu as pltpu
from jax.sharding import PartitionSpec as P

beta_coef = 1.0 / 3.0
near_coef = 7.0 / 9.0
far_coef = 1.0 / 36.0
time_step = 0.4
highest = lax.Precision.HIGHEST
vmem_bytes = 63 * 1024 * 1024


def line_matrices(length):
    matrix = np.eye(length) + beta_coef * (np.eye(length, k=1) + np.eye(length, k=-1))
    rows = np.arange(length)
    spread = np.zeros((length, length + 4))
    spread[rows, rows + 3] += near_coef
    spread[rows, rows + 1] -= near_coef
    spread[rows, rows + 4] += far_coef
    spread[rows, rows] -= far_coef
    return np.linalg.inv(matrix), spread


def scaled_rows(table, diagonal):
    rows, width = table.shape
    reach = np.clip(np.asarray(diagonal)[:, None] + np.arange(-14, 15)[None, :], -1, width)
    padded = np.concatenate([np.zeros((rows, 1)), table, np.zeros((rows, 1))], axis=1)
    near, which = np.unique(
        np.round(np.take_along_axis(padded, reach + 1, axis=1), 12), axis=0, return_inverse=True
    )
    scales = np.exp2(np.arange(4096) / 4096.0)
    best = np.zeros(near.shape[0])
    for i, row in enumerate(near):
        tried = row[None, :] / scales[:, None]
        error = tried.astype(np.float32).astype(jnp.bfloat16).astype(np.float64) - tried
        best[i] = scales[np.argmin(np.sum(np.square(error * scales[:, None]), axis=1))]
    scale = best[which.reshape(-1)].astype(np.float32).astype(np.float64)
    values = (table / scale[:, None]).astype(np.float32).astype(jnp.bfloat16)
    return scale, values.astype(np.float32)


def block_tables(cells, groups):
    length = cells * groups
    inverse, spread = line_matrices(length)
    whole = -time_step * inverse @ spread[:, 2:-2]
    own = np.zeros((groups, cells, cells))
    beyond = np.zeros((groups, 4, cells))
    act = np.zeros((groups, 4, cells))
    for g in range(groups):
        s, e = g * cells, (g + 1) * cells
        own[g] = whole[s:e, s:e]
        if g > 0:
            beyond[g, 0] = whole[s - 1, s:e]
            beyond[g, 1] = whole[s - 2, s:e]
            act[g, 0, 0] = 1.0
            act[g, 1, 1:] = inverse[s + 1 : e, s] / inverse[s + 1, s]
        if g < groups - 1:
            beyond[g, 2] = whole[e, s:e]
            beyond[g, 3] = whole[e + 1, s:e]
            act[g, 2, cells - 1] = 1.0
            act[g, 3, : cells - 1] = inverse[s : e - 1, e - 1] / inverse[e - 2, e - 1]
    return own, beyond, act


def edge_scalars(beyond, cells):
    groups = beyond.shape[0]
    table = np.zeros((groups, 2 * cells + 4))
    table[:, :cells] = beyond[:, 1]
    table[:, cells : 2 * cells] = beyond[:, 3]
    for g in range(groups):
        if g > 0:
            table[g, 2 * cells] = beyond[g, 0, 1] / beyond[g, 1, 1]
            table[g, 2 * cells + 1] = beyond[g, 0, 0] - table[g, 2 * cells] * beyond[g, 1, 0]
        if g < groups - 1:
            table[g, 2 * cells + 2] = beyond[g, 2, cells - 2] / beyond[g, 3, cells - 2]
            table[g, 2 * cells + 3] = (
                beyond[g, 2, cells - 1] - table[g, 2 * cells + 2] * beyond[g, 3, cells - 1]
            )
    return table


def common(fields):
    rho, m1, m2, m3, energy = fields
    inv = 1.0 / rho
    pressure = 0.4 * (energy - 0.5 * inv * (m1 * m1 + m2 * m2 + m3 * m3))
    return inv, pressure, energy + pressure


def flux_from(fields, shared, direction):
    inv, pressure, total = shared
    velocity = fields[1 + direction] * inv
    out = [fields[1 + direction]]
    for component in range(3):
        term = fields[1 + component] * velocity
        out.append(term + pressure if component == direction else term)
    out.append(total * velocity)
    return out


def load_fields(rho, mom, ene, idx):
    return [rho[idx], mom[(0,) + idx], mom[(1,) + idx], mom[(2,) + idx], ene[idx]]


def split(value):
    high = value.astype(jnp.bfloat16)
    return high, (value - high.astype(jnp.float32)).astype(jnp.bfloat16)


def ghost_copies(sent, got, send_sem, recv_sem, groups):
    me = lax.axis_index("gx")
    cap = sent.shape[0] // groups
    copies = []
    for off in range(1, groups):
        target = lax.rem(me + off, groups)
        copies.append(
            pltpu.make_async_remote_copy(
                src_ref=sent.at[pl.ds(pl.multiple_of(target * cap, cap), cap)],
                dst_ref=got.at[pl.ds(pl.multiple_of(me * cap, cap), cap)],
                send_sem=send_sem.at[off],
                recv_sem=recv_sem.at[off],
                device_id={"gx": target},
                device_id_type=pl.DeviceIdType.MESH,
            )
        )
    return copies


def up_to(slots):
    row = lax.broadcasted_iota(jnp.int32, (slots, slots), 0)
    return jnp.where(row <= lax.broadcasted_iota(jnp.int32, (slots, slots), 1), 1.0, 0.0)


def send_ghosts(rows_ref, time_ref, coarse, sent, got, send_sem, recv_sem, groups):
    me = lax.axis_index("gx")
    slots = rows_ref.shape[1]
    block = coarse.shape[2]
    cap = slots // groups
    f32 = jnp.float32
    highest_dot = functools.partial(
        lax.dot_general, precision=highest, preferred_element_type=f32
    )
    barrier = pltpu.get_barrier_semaphore()
    for off in range(1, groups):
        pl.semaphore_signal(
            barrier, inc=1, device_id={"gx": lax.rem(me + off, groups)}, device_id_type=pl.DeviceIdType.MESH
        )

    rows = rows_ref[...]
    first = me * block
    mine = jnp.where((rows >= first) & (rows < first + block), 1.0, 0.0)
    upper = up_to(slots)
    rank = jnp.where(mine > 0.5, jnp.dot(mine, upper, preferred_element_type=f32) - 1.0, -1.0)
    wanted = lax.broadcasted_iota(jnp.int32, (cap, slots), 0).astype(f32)
    local_rows = (rows - first).astype(f32)
    level = time_ref[...].astype(f32) * 0.125
    picked, levels = [], []
    for a in range(groups):
        pick = rank[a : a + 1] == wanted
        picked.append(jnp.sum(jnp.where(pick, local_rows[a : a + 1], 0.0), axis=1, keepdims=True))
        levels.append(jnp.sum(jnp.where(pick, level[a : a + 1], 0.0), axis=1, keepdims=True))
    picked = jnp.concatenate(picked, axis=0)
    levels = jnp.concatenate(levels, axis=0)
    onehot = jnp.where(
        picked == lax.broadcasted_iota(jnp.int32, (slots, block), 1).astype(f32), 1.0, 0.0
    )
    contract = (((1,), (1,)), ((), ()))
    old = highest_dot(onehot, coarse[0], contract)
    new = highest_dot(onehot, coarse[1], contract)
    sent[...] = (1.0 - levels) * old + levels * new

    pl.semaphore_wait(barrier, groups - 1)
    for copy in ghost_copies(sent, got, send_sem, recv_sem, groups):
        copy.start()
    here = pl.ds(pl.multiple_of(me * cap, cap), cap)
    got[here] = sent[here]


def finish_ghosts(rows_ref, block, out, sent, got, send_sem, recv_sem, groups, cells):
    me = lax.axis_index("gx")
    slots = rows_ref.shape[1]
    cap = slots // groups
    f32 = jnp.float32
    highest_dot = functools.partial(
        lax.dot_general, precision=highest, preferred_element_type=f32
    )
    upper = up_to(slots)
    own = rows_ref[pl.ds(me, 1)]
    source = lax.broadcasted_iota(jnp.int32, (groups, slots), 0) * block
    match = jnp.where((own >= source) & (own < source + block), 1.0, 0.0)
    nth = jnp.dot(match, upper, preferred_element_type=f32) - 1.0
    base = lax.broadcasted_iota(jnp.int32, (groups, slots), 0).astype(f32) * cap
    index = jnp.sum(match * (nth + base), axis=0, keepdims=True)
    back = jnp.where(lax.broadcasted_iota(jnp.int32, (slots, slots), 0).astype(f32) == index, 1.0, 0.0)
    for copy in ghost_copies(sent, got, send_sem, recv_sem, groups):
        copy.wait()
    ghosts = highest_dot(got[...], back, (((0,), (0,)), ((), ())))
    fields = [ghosts[f * cells : (f + 1) * cells] for f in range(5)]
    for f, value in enumerate(flux_from(fields, common(fields), 2)):
        out[f] = value


def edge_kernel(
    cx, cy, weights, rows, times, coarse, rho, mom, ene, xlo, xhi, ylo, yhi, hg,
    ysum, sent, got, send_sem, recv_sem, *, cells, tile, last, groups
):
    step = pl.program_id(0)
    px, py = lax.axis_index("gx"), lax.axis_index("gy")
    zs = rho.shape[2] // 128

    @pl.when(step == 0)
    def _():
        send_ghosts(rows, times, coarse, sent, got, send_sem, recv_sem, groups)
        xlo[...] = jnp.zeros_like(xlo)
        xhi[...] = jnp.zeros_like(xhi)

    def piece(n, _):
        zc = pl.ds(pl.multiple_of(n * 128, 128), 128)
        for yy in range(0, cells, 16):
            ys = pl.ds(yy, 16)
            low = [xlo[f, 1, ys, zc] for f in range(5)]
            high = [xhi[f, 1, ys, zc] for f in range(5)]
            for x in range(tile):
                fields = load_fields(rho, mom, ene, (x, ys, zc))
                shared = common(fields)
                flux = flux_from(fields, shared, 0)
                cl = cx[px, step * tile + x]
                ch = cx[px, cells + step * tile + x]
                for f in range(5):
                    low[f] += cl * flux[f]
                    high[f] += ch * flux[f]
                if x == 0:
                    first = flux

                    @pl.when(step == 0)
                    def _():
                        for f in range(5):
                            xlo[f, 0, ys, zc] = cx[px, 2 * cells + 1] * first[f]

                if x == tile - 1:
                    end = flux

                    @pl.when(step == last)
                    def _():
                        for f in range(5):
                            xhi[f, 0, ys, zc] = cx[px, 2 * cells + 3] * end[f]

                side = flux_from(fields, shared, 1)
                row = pl.ds(x, 1)
                for f in range(5):
                    for d, out in ((0, ylo), (1, yhi)):
                        part = side[f] * weights[py, d, ys]
                        part = part[:8] + part[8:]
                        if yy > 0:
                            part += ysum[f, d, x]
                        if yy + 16 < cells:
                            ysum[f, d, x] = part
                        else:
                            total = jnp.sum(part, axis=0, keepdims=True)
                            out[f, 1, row, zc] = total
                            if d == 0:
                                out[f, 0, row, zc] += cy[py, 2 * cells] * total
                            else:
                                out[f, 0, row, zc] = (
                                    cy[py, 2 * cells + 2] * total + cy[py, 2 * cells + 3] * side[f][15:]
                                )
                    if yy == 0:
                        ylo[f, 0, row, zc] = cy[py, 2 * cells + 1] * side[f][:1]
            for f in range(5):
                xlo[f, 1, ys, zc] = low[f]
                xhi[f, 1, ys, zc] = high[f]

            @pl.when(step == last)
            def _():
                for f in range(5):
                    xlo[f, 0, ys, zc] += cx[px, 2 * cells] * low[f]
                    xhi[f, 0, ys, zc] += cx[px, 2 * cells + 2] * high[f]

        return 0

    lax.fori_loop(0, zs, piece, 0)

    @pl.when(step == last)
    def _():
        finish_ghosts(rows, coarse.shape[2], hg, sent, got, send_sem, recv_sem, groups, cells)


def lines_kernel(
    mx, my, mz, wz, sx, sy, sz, hg, to_low_x, to_high_x, to_low_y, to_high_y, rho, mom, ene,
    out, low_x, high_x, low_y, high_y, send_sem, recv_sem, keep_sem,
    f_buf, g_buf, h_buf, acc, mx_buf, my_buf, mz_buf, *, cells, tile, steps
):
    step = pl.program_id(0)
    width = rho.shape[2]
    zs = width // 128
    rows = tile * cells
    bf16 = jnp.bfloat16
    dot = functools.partial(jnp.dot, preferred_element_type=jnp.float32)
    chunks = [(z * 128, (z + 1) * 128) for z in range(zs)]

    moves = []
    for n, (axis, by, source, target) in enumerate(
        (("gx", 1, to_high_x, low_x), ("gx", -1, to_low_x, high_x),
         ("gy", 1, to_high_y, low_y), ("gy", -1, to_low_y, high_y))
    ):
        here, count = lax.axis_index(axis), lax.axis_size(axis)
        sends = here < count - 1 if by > 0 else here > 0
        gets = here > 0 if by > 0 else here < count - 1
        copy = pltpu.make_async_remote_copy(
            src_ref=source, dst_ref=target, send_sem=send_sem.at[n], recv_sem=recv_sem.at[n],
            device_id={axis: jnp.clip(here + by, 0, count - 1)}, device_id_type=pl.DeviceIdType.MESH,
        )
        own = pltpu.make_async_copy(source, target, keep_sem.at[n])
        moves.append((axis, here + by, sends, gets, copy, own))

    @pl.when(step == 0)
    def _():
        barrier = pltpu.get_barrier_semaphore()
        for axis, to, sends, _, _, _ in moves:
            @pl.when(sends)
            def _():
                pl.semaphore_signal(
                    barrier, inc=1, device_id={axis: to}, device_id_type=pl.DeviceIdType.MESH
                )
        pl.semaphore_wait(barrier, sum(jnp.where(gets, 1, 0) for _, _, _, gets, _, _ in moves))
        for _, _, sends, gets, copy, own in moves:
            @pl.when(sends)
            def _():
                copy.start()

            @pl.when(jnp.logical_not(gets))
            def _():
                own.start()
        for buf, table in ((mx_buf, mx[lax.axis_index("gx")]), (my_buf, my[lax.axis_index("gy")])):
            buf[:, :rows] = table.astype(bf16)
            buf[:, rows:] = table.astype(bf16)
        mz_buf[...] = mz[...].astype(bf16)

    @pl.when(step < steps)
    def _():
        def piece(n, _):
            x = (n // (2 * zs)) * 2
            yy = pl.multiple_of((n // zs) % 2 * 16, 16)
            zc = pl.multiple_of((n % zs) * 128, 128)
            z_hi, z_lo = pl.ds(zc, 128), pl.ds(width + zc, 128)
            fields = load_fields(rho, mom, ene, (pl.ds(x, 2), pl.ds(yy, 16), z_hi))
            shared = common(fields)
            for f, value in enumerate(flux_from(fields, shared, 0)):
                for j in range(2):
                    hi, lo = split(value[:, 8 * j : 8 * j + 8].reshape(16, 128))
                    at = pl.multiple_of((step * tile + x) * 8, 16)
                    f_buf[yy // 8 + j, f, pl.ds(at, 16), z_hi] = hi
                    f_buf[yy // 8 + j, f, pl.ds(cells * 8 + at, 16), z_hi] = lo
            for f, value in enumerate(flux_from(fields, shared, 1)):
                for j in range(2):
                    hi, lo = split(value[j])
                    at = pl.multiple_of((x + j) * cells + yy, 16)
                    g_buf[f, pl.ds(at, 16), z_hi] = hi
                    g_buf[f, pl.ds(rows + at, 16), z_hi] = lo
            for f, value in enumerate(flux_from(fields, shared, 2)):
                for j in range(2):
                    hi, lo = split(value[j])
                    at = pl.multiple_of((x + j) * cells + yy, 16)
                    h_buf[f, pl.ds(at, 16), z_hi] = hi
                    h_buf[f, pl.ds(at, 16), z_lo] = lo
            return 0

        lax.fori_loop(0, (tile // 2) * 2 * zs, piece, 0)
        half = width // 2
        slots = hg.shape[2]
        own_slot = jnp.where(
            lax.broadcasted_iota(jnp.int32, (rows, slots), 1) % cells
            == lax.broadcasted_iota(jnp.int32, (rows, slots), 0) // cells + step * tile,
            1.0, 0.0,
        )
        for f in range(5):
            base = rho if f == 0 else ene if f == 4 else mom.at[f - 1]
            y_part = dot(my_buf[...], g_buf[f])
            g_hi, g_lo = split(jnp.concatenate([hg[f]] * tile, axis=0) * own_slot)
            ghost = jnp.concatenate([g_hi, g_lo], axis=1)
            for k in range(2):
                low = 0 if k == 0 else half - 128
                high = half + 128 if k == 0 else width
                left = jnp.concatenate([h_buf[f, :, low:high], h_buf[f, :, width + low : width + high]], axis=1)
                weight = mz_buf[low:high, k * half : (k + 1) * half]
                z_part = dot(left, jnp.concatenate([weight, weight], axis=0))
                edge = slice(0, 128) if k == 0 else slice(width - 128, width)
                ends = dot(ghost, wz[:, edge].astype(bf16))
                for a, b in chunks[k * zs // 2 : (k + 1) * zs // 2]:
                    got = z_part[:, a - k * half : b - k * half]
                    if a == edge.start:
                        got = got + ends
                    got = got * sz[:, a:b] + y_part[:, a:b] * sy[lax.axis_index("gy")]
                    acc[f, pl.ds(step * tile, tile), :, a:b] = base[:, :, a:b] + got.reshape(tile, cells, 128)

    @pl.when(step >= steps)
    def _():
        j = step - steps
        at = pl.multiple_of(j * 8, 8)
        for f in range(5):
            got = dot(mx_buf[...], f_buf[j, f])
            for a, b in chunks:
                part = (got[:, a:b] * sx[lax.axis_index("gx")]).reshape(cells, 8, 128)
                out[f, :, :, a:b] = acc[f, :, pl.ds(at, 8), a:b] + part

    @pl.when(step == 2 * steps - 1)
    def _():
        for _, _, sends, gets, copy, own in moves:
            @pl.when(sends)
            def _():
                copy.wait_send()

            @pl.when(gets)
            def _():
                copy.wait_recv()

            @pl.when(jnp.logical_not(gets))
            def _():
                own.wait()


def join_kernel(place, ax, ay, acc, xlo, xhi, ylo, yhi, out, *, cells, tile, last, groups):
    step = pl.program_id(0)
    px = place[0]
    zs = acc.shape[3] // 128

    def piece(n, _):
        zc = pl.ds(pl.multiple_of(n * 128, 128), 128)
        weights = [(ax[px, step * tile + x], ax[px, cells + step * tile + x]) for x in range(tile)]
        for yy in range(0, cells, 8):
            ys = slice(yy, yy + 8)
            a_low, a_high = ay[0, 1, ys], ay[0, 3, ys]
            for f in range(5):
                x_low, x_high = xlo[f, 1, ys, zc], xhi[f, 1, ys, zc]
                for x in range(tile):
                    row = slice(x, x + 1)
                    term = acc[f, x, ys, zc] + weights[x][0] * x_low + weights[x][1] * x_high
                    term += a_low * ylo[f, 1, row, zc] + a_high * yhi[f, 1, row, zc]
                    if yy == 0:
                        term += ay[0, 0, ys] * ylo[f, 0, row, zc]
                    if yy + 8 == cells:
                        term += ay[0, 2, ys] * yhi[f, 0, row, zc]
                    out[f, x, ys, zc] = term
        return 0

    lax.fori_loop(0, zs, piece, 0)

    @pl.when((step == 0) & (px > 0))
    def _():
        for f in range(5):
            out[f, 0] += xlo[f, 0]

    @pl.when((step == last) & (px < groups - 1))
    def _():
        for f in range(5):
            out[f, tile - 1] += xhi[f, 0]


def local(density, momentum, energy, coarse_rows, ghost_rows, time_index):
    cells, _, cells_z = density.shape
    groups_x, groups_y = lax.axis_size("gx"), lax.axis_size("gy")
    place_x, place_y = lax.axis_index("gx"), lax.axis_index("gy")
    place = jnp.stack([place_x, place_y]).astype(jnp.int32)
    tile = 8
    steps = cells // tile
    f32 = jnp.float32

    own_x, beyond_x, act_x = block_tables(cells, groups_x)
    own_y, beyond_y, act_y = block_tables(cells, groups_y)
    inverse_z, spread_z = line_matrices(cells_z)
    whole_z = -time_step * inverse_z @ spread_z
    at_x = np.tile(np.arange(cells), groups_x)
    at_y = np.tile(np.arange(cells), groups_y)
    scale_x, values_x = scaled_rows(own_x.reshape(-1, cells), at_x)
    scale_y, values_y = scaled_rows(own_y.reshape(-1, cells), at_y)
    scale_z, values_z = scaled_rows(whole_z, np.arange(cells_z) + 2)
    lanes = np.ones((1, 128), np.float32)
    mx = np.stack([np.kron(m, np.eye(8)) for m in values_x.reshape(own_x.shape)]).astype(np.float32)
    my = np.stack([np.kron(np.eye(tile), m) for m in values_y.reshape(own_y.shape)]).astype(np.float32)
    mz = np.ascontiguousarray(values_z[:, 2:-2].T)
    sx = np.stack([np.repeat(v, 8)[:, None] * lanes for v in scale_x.reshape(groups_x, cells)])
    sy = np.stack([np.tile(v, tile)[:, None] * lanes for v in scale_y.reshape(groups_y, cells)])
    sx, sy, sz = sx.astype(np.float32), sy.astype(np.float32), scale_z[None, :].astype(np.float32)
    wz = np.tile(np.repeat(values_z[:, [0, 1, cells_z + 2, cells_z + 3]].T, cells, axis=0), (2, 1))
    cy = edge_scalars(beyond_y, cells).astype(np.float32)
    weights = np.broadcast_to(beyond_y[:, 1::2, :, None], (groups_y, 2, cells, 128)).astype(np.float32)
    cx = edge_scalars(beyond_x, cells).astype(np.float32)
    ax = np.concatenate([act_x[:, 1], act_x[:, 3]], axis=1).astype(np.float32)
    ay = np.broadcast_to(act_y[..., None], act_y.shape + (128,)).astype(np.float32)


    smem = pl.BlockSpec(memory_space=pltpu.SMEM)
    anywhere = pl.BlockSpec(memory_space=pl.ANY)
    planes = jax.ShapeDtypeStruct((5, 2, cells, cells_z), f32)
    whole = jax.ShapeDtypeStruct((5, cells, cells, cells_z), f32)
    size = 4 * 5 * cells * cells * cells_z
    rows = tile * cells
    bf16 = jnp.bfloat16
    top = steps - 1

    def spec(dims, axis=None, index=lambda i: i):
        def place_of(i, *_):
            return tuple(index(i) if d == axis else 0 for d in range(len(dims)))

        return pl.BlockSpec(dims, place_of)

    def fixed(table):
        return spec(table.shape)

    def state_specs(index):
        return [
            spec((tile, cells, cells_z), 0, index),
            spec((3, tile, cells, cells_z), 1, index),
            spec((tile, cells, cells_z), 0, index),
        ]

    def params(**more):
        return pltpu.CompilerParams(
            vmem_limit_bytes=vmem_bytes, dimension_semantics=("arbitrary",), **more
        )

    def cost(flops, moved):
        return pl.CostEstimate(flops=flops, bytes_accessed=moved, transcendentals=0)

    slots, width = ghost_rows.shape[2], coarse_rows.shape[3]
    coarse = coarse_rows[:, :, 0, :].transpose(0, 2, 1)
    same = lambda i: i
    xlo, xhi, ylo, yhi, hg = pl.pallas_call(
        functools.partial(edge_kernel, cells=cells, tile=tile, last=top, groups=groups_x),
        grid=(steps,),
        in_specs=[
            smem, smem, fixed(weights), fixed(ghost_rows[0]), fixed(time_index[0]), fixed(coarse),
            *state_specs(same),
        ],
        out_shape=[planes] * 4 + [jax.ShapeDtypeStruct((5, cells, slots), f32)],
        out_specs=[
            spec(planes.shape), spec(planes.shape),
            spec((5, 2, tile, cells_z), 2), spec((5, 2, tile, cells_z), 2), spec((5, cells, slots)),
        ],
        scratch_shapes=[
            pltpu.VMEM((5, 2, tile, 8, 128), f32),
            pltpu.VMEM((slots, width), f32),
            pltpu.VMEM((slots, width), f32),
            pltpu.SemaphoreType.DMA((groups_x,)),
            pltpu.SemaphoreType.DMA((groups_x,)),
        ],
        compiler_params=params(collective_id=0, has_side_effects=True),
        cost_estimate=cost(size * 20, size),
        name="edges",
    )(cx, cy, weights, ghost_rows[0], time_index[0], coarse, density, momentum, energy)

    acc, in_xlo, in_xhi, in_ylo, in_yhi = pl.pallas_call(
        functools.partial(lines_kernel, cells=cells, tile=tile, steps=steps),
        grid=(2 * steps,),
        in_specs=[
            fixed(mx), fixed(my), fixed(mz), fixed(wz), fixed(sx), fixed(sy), fixed(sz), fixed(hg),
            *[anywhere] * 4, *state_specs(lambda i: jnp.minimum(i, top)),
        ],
        out_shape=[whole] + [planes] * 4,
        out_specs=[
            spec((5, cells, 8, cells_z), 2, lambda i: jnp.maximum(i - steps, 0)), *[anywhere] * 4
        ],
        scratch_shapes=[
            pltpu.SemaphoreType.DMA((4,)),
            pltpu.SemaphoreType.DMA((4,)),
            pltpu.SemaphoreType.DMA((4,)),
            pltpu.VMEM((cells // 8, 5, 2 * cells * 8, cells_z), bf16),
            pltpu.VMEM((5, 2 * rows, cells_z), bf16),
            pltpu.VMEM((5, rows, 2 * cells_z), bf16),
            pltpu.VMEM((5, cells, cells, cells_z), f32),
            pltpu.VMEM((cells * 8, 2 * cells * 8), bf16),
            pltpu.VMEM((rows, 2 * rows), bf16),
            pltpu.VMEM((cells_z, cells_z), bf16),
        ],
        compiler_params=params(collective_id=1, has_side_effects=True),
        cost_estimate=cost(size * 1200, 2 * size),
        name="lines",
    )(mx, my, mz, wz, sx, sy, sz, hg, xlo, xhi, ylo, yhi, density, momentum, energy)

    return pl.pallas_call(
        functools.partial(join_kernel, cells=cells, tile=tile, last=top, groups=groups_x),
        grid_spec=pltpu.PrefetchScalarGridSpec(
            num_scalar_prefetch=1,
            grid=(steps,),
            in_specs=[
                smem, pl.BlockSpec((1, *ay.shape[1:]), lambda i, p: (p[1], 0, 0, 0)),
                spec((5, tile, cells, cells_z), 1), spec(planes.shape), spec(planes.shape),
                spec((5, 2, tile, cells_z), 2), spec((5, 2, tile, cells_z), 2),
            ],
            out_specs=spec((5, tile, cells, cells_z), 1),
        ),
        out_shape=whole,
        compiler_params=params(),
        cost_estimate=cost(size * 4, 2 * size),
        name="join",
    )(place, ax, ay, acc, in_xlo, in_xhi, in_ylo, in_yhi)


def solution(mesh):
    return jax.shard_map(
        local,
        mesh=mesh,
        in_specs=(
            P("gx", "gy", None),
            P(None, "gx", "gy", None),
            P("gx", "gy", None),
            P(None, "gx", "gy", None),
            P("gy", None, None),
            P("gy", None, None),
        ),
        out_specs=P(None, "gx", "gy", None),
        check_vma=False,
    )
```

```python
import functools

import jax
import jax.numpy as jnp
import numpy as np
from jax import lax
from jax.experimental import pallas as pl
from jax.experimental.pallas import tpu as pltpu
from jax.sharding import PartitionSpec as P

beta_coef = 1.0 / 3.0
near_coef = 7.0 / 9.0
far_coef = 1.0 / 36.0
time_step = 0.4
highest = lax.Precision.HIGHEST
vmem_bytes = 63 * 1024 * 1024


def line_matrices(length):
    matrix = np.eye(length) + beta_coef * (np.eye(length, k=1) + np.eye(length, k=-1))
    rows = np.arange(length)
    spread = np.zeros((length, length + 4))
    spread[rows, rows + 3] += near_coef
    spread[rows, rows + 1] -= near_coef
    spread[rows, rows + 4] += far_coef
    spread[rows, rows] -= far_coef
    return np.linalg.inv(matrix), spread


def scaled_rows(table, diagonal):
    rows, width = table.shape
    reach = np.clip(np.asarray(diagonal)[:, None] + np.arange(-14, 15)[None, :], -1, width)
    padded = np.concatenate([np.zeros((rows, 1)), table, np.zeros((rows, 1))], axis=1)
    near, which = np.unique(
        np.round(np.take_along_axis(padded, reach + 1, axis=1), 12), axis=0, return_inverse=True
    )
    scales = np.exp2(np.arange(4096) / 4096.0)
    best = np.zeros(near.shape[0])
    for i, row in enumerate(near):
        tried = row[None, :] / scales[:, None]
        error = tried.astype(np.float32).astype(jnp.bfloat16).astype(np.float64) - tried
        best[i] = scales[np.argmin(np.sum(np.square(error * scales[:, None]), axis=1))]
    scale = best[which.reshape(-1)].astype(np.float32).astype(np.float64)
    values = (table / scale[:, None]).astype(np.float32).astype(jnp.bfloat16)
    return scale, values.astype(np.float32)


def block_tables(cells, groups):
    length = cells * groups
    inverse, spread = line_matrices(length)
    whole = -time_step * inverse @ spread[:, 2:-2]
    own = np.zeros((groups, cells, cells))
    beyond = np.zeros((groups, 4, cells))
    act = np.zeros((groups, 4, cells))
    for g in range(groups):
        s, e = g * cells, (g + 1) * cells
        own[g] = whole[s:e, s:e]
        if g > 0:
            beyond[g, 0] = whole[s - 1, s:e]
            beyond[g, 1] = whole[s - 2, s:e]
            act[g, 0, 0] = 1.0
            act[g, 1, 1:] = inverse[s + 1 : e, s] / inverse[s + 1, s]
        if g < groups - 1:
            beyond[g, 2] = whole[e, s:e]
            beyond[g, 3] = whole[e + 1, s:e]
            act[g, 2, cells - 1] = 1.0
            act[g, 3, : cells - 1] = inverse[s : e - 1, e - 1] / inverse[e - 2, e - 1]
    return own, beyond, act


def edge_scalars(beyond, cells):
    groups = beyond.shape[0]
    table = np.zeros((groups, 2 * cells + 4))
    table[:, :cells] = beyond[:, 1]
    table[:, cells : 2 * cells] = beyond[:, 3]
    for g in range(groups):
        if g > 0:
            table[g, 2 * cells] = beyond[g, 0, 1] / beyond[g, 1, 1]
            table[g, 2 * cells + 1] = beyond[g, 0, 0] - table[g, 2 * cells] * beyond[g, 1, 0]
        if g < groups - 1:
            table[g, 2 * cells + 2] = beyond[g, 2, cells - 2] / beyond[g, 3, cells - 2]
            table[g, 2 * cells + 3] = (
                beyond[g, 2, cells - 1] - table[g, 2 * cells + 2] * beyond[g, 3, cells - 1]
            )
    return table


def common(fields):
    rho, m1, m2, m3, energy = fields
    inv = 1.0 / rho
    pressure = 0.4 * (energy - 0.5 * inv * (m1 * m1 + m2 * m2 + m3 * m3))
    return inv, pressure, energy + pressure


def flux_from(fields, shared, direction):
    inv, pressure, total = shared
    velocity = fields[1 + direction] * inv
    out = [fields[1 + direction]]
    for component in range(3):
        term = fields[1 + component] * velocity
        out.append(term + pressure if component == direction else term)
    out.append(total * velocity)
    return out


def load_fields(rho, mom, ene, idx):
    return [rho[idx], mom[(0,) + idx], mom[(1,) + idx], mom[(2,) + idx], ene[idx]]


def split(value):
    high = value.astype(jnp.bfloat16)
    return high, (value - high.astype(jnp.float32)).astype(jnp.bfloat16)


def ghost_copies(sent, got, send_sem, recv_sem, groups):
    me = lax.axis_index("gx")
    cap = sent.shape[0] // groups
    copies = []
    for off in range(1, groups):
        target = lax.rem(me + off, groups)
        copies.append(
            pltpu.make_async_remote_copy(
                src_ref=sent.at[pl.ds(pl.multiple_of(target * cap, cap), cap)],
                dst_ref=got.at[pl.ds(pl.multiple_of(me * cap, cap), cap)],
                send_sem=send_sem.at[off],
                recv_sem=recv_sem.at[off],
                device_id={"gx": target},
                device_id_type=pl.DeviceIdType.MESH,
            )
        )
    return copies


def up_to(slots):
    row = lax.broadcasted_iota(jnp.int32, (slots, slots), 0)
    return jnp.where(row <= lax.broadcasted_iota(jnp.int32, (slots, slots), 1), 1.0, 0.0)


def send_ghosts(rows_ref, time_ref, coarse, sent, got, send_sem, recv_sem, groups):
    me = lax.axis_index("gx")
    slots = rows_ref.shape[1]
    block = coarse.shape[2]
    cap = slots // groups
    f32 = jnp.float32
    highest_dot = functools.partial(
        lax.dot_general, precision=highest, preferred_element_type=f32
    )
    barrier = pltpu.get_barrier_semaphore()
    for off in range(1, groups):
        pl.semaphore_signal(
            barrier, inc=1, device_id={"gx": lax.rem(me + off, groups)}, device_id_type=pl.DeviceIdType.MESH
        )

    rows = rows_ref[...]
    first = me * block
    mine = jnp.where((rows >= first) & (rows < first + block), 1.0, 0.0)
    upper = up_to(slots)
    rank = jnp.where(mine > 0.5, jnp.dot(mine, upper, preferred_element_type=f32) - 1.0, -1.0)
    wanted = lax.broadcasted_iota(jnp.int32, (cap, slots), 0).astype(f32)
    local_rows = (rows - first).astype(f32)
    level = time_ref[...].astype(f32) * 0.125
    picked, levels = [], []
    for a in range(groups):
        pick = rank[a : a + 1] == wanted
        picked.append(jnp.sum(jnp.where(pick, local_rows[a : a + 1], 0.0), axis=1, keepdims=True))
        levels.append(jnp.sum(jnp.where(pick, level[a : a + 1], 0.0), axis=1, keepdims=True))
    picked = jnp.concatenate(picked, axis=0)
    levels = jnp.concatenate(levels, axis=0)
    onehot = jnp.where(
        picked == lax.broadcasted_iota(jnp.int32, (slots, block), 1).astype(f32), 1.0, 0.0
    )
    contract = (((1,), (1,)), ((), ()))
    old = highest_dot(onehot, coarse[0], contract)
    new = highest_dot(onehot, coarse[1], contract)
    sent[...] = (1.0 - levels) * old + levels * new

    pl.semaphore_wait(barrier, groups - 1)
    for copy in ghost_copies(sent, got, send_sem, recv_sem, groups):
        copy.start()
    here = pl.ds(pl.multiple_of(me * cap, cap), cap)
    got[here] = sent[here]


def finish_ghosts(rows_ref, block, out, sent, got, send_sem, recv_sem, groups, cells):
    me = lax.axis_index("gx")
    slots = rows_ref.shape[1]
    cap = slots // groups
    f32 = jnp.float32
    highest_dot = functools.partial(
        lax.dot_general, precision=highest, preferred_element_type=f32
    )
    upper = up_to(slots)
    own = rows_ref[pl.ds(me, 1)]
    source = lax.broadcasted_iota(jnp.int32, (groups, slots), 0) * block
    match = jnp.where((own >= source) & (own < source + block), 1.0, 0.0)
    nth = jnp.dot(match, upper, preferred_element_type=f32) - 1.0
    base = lax.broadcasted_iota(jnp.int32, (groups, slots), 0).astype(f32) * cap
    index = jnp.sum(match * (nth + base), axis=0, keepdims=True)
    back = jnp.where(lax.broadcasted_iota(jnp.int32, (slots, slots), 0).astype(f32) == index, 1.0, 0.0)
    for copy in ghost_copies(sent, got, send_sem, recv_sem, groups):
        copy.wait()
    ghosts = highest_dot(got[...], back, (((0,), (0,)), ((), ())))
    fields = [ghosts[f * cells : (f + 1) * cells] for f in range(5)]
    for f, value in enumerate(flux_from(fields, common(fields), 2)):
        out[f] = value


def edge_kernel(
    cx, cy, weights, rows, times, coarse, rho, mom, ene, xlo, xhi, ylo, yhi, hg,
    ysum, sent, got, send_sem, recv_sem, *, cells, tile, last, groups
):
    step = pl.program_id(0)
    px, py = lax.axis_index("gx"), lax.axis_index("gy")
    zs = rho.shape[2] // 128

    @pl.when(step == 0)
    def _():
        send_ghosts(rows, times, coarse, sent, got, send_sem, recv_sem, groups)
        xlo[...] = jnp.zeros_like(xlo)
        xhi[...] = jnp.zeros_like(xhi)

    def piece(n, _):
        zc = pl.ds(pl.multiple_of(n * 128, 128), 128)
        for yy in range(0, cells, 16):
            ys = pl.ds(yy, 16)
            low = [xlo[f, 1, ys, zc] for f in range(5)]
            high = [xhi[f, 1, ys, zc] for f in range(5)]
            for x in range(tile):
                fields = load_fields(rho, mom, ene, (x, ys, zc))
                shared = common(fields)
                flux = flux_from(fields, shared, 0)
                cl = cx[px, step * tile + x]
                ch = cx[px, cells + step * tile + x]
                for f in range(5):
                    low[f] += cl * flux[f]
                    high[f] += ch * flux[f]
                if x == 0:
                    first = flux

                    @pl.when(step == 0)
                    def _():
                        for f in range(5):
                            xlo[f, 0, ys, zc] = cx[px, 2 * cells + 1] * first[f]

                if x == tile - 1:
                    end = flux

                    @pl.when(step == last)
                    def _():
                        for f in range(5):
                            xhi[f, 0, ys, zc] = cx[px, 2 * cells + 3] * end[f]

                side = flux_from(fields, shared, 1)
                row = pl.ds(x, 1)
                for f in range(5):
                    for d, out in ((0, ylo), (1, yhi)):
                        part = side[f] * weights[py, d, ys]
                        part = part[:8] + part[8:]
                        if yy > 0:
                            part += ysum[f, d, x]
                        if yy + 16 < cells:
                            ysum[f, d, x] = part
                        else:
                            total = jnp.sum(part, axis=0, keepdims=True)
                            out[f, 1, row, zc] = total
                            if d == 0:
                                out[f, 0, row, zc] += cy[py, 2 * cells] * total
                            else:
                                out[f, 0, row, zc] = (
                                    cy[py, 2 * cells + 2] * total + cy[py, 2 * cells + 3] * side[f][15:]
                                )
                    if yy == 0:
                        ylo[f, 0, row, zc] = cy[py, 2 * cells + 1] * side[f][:1]
            for f in range(5):
                xlo[f, 1, ys, zc] = low[f]
                xhi[f, 1, ys, zc] = high[f]

            @pl.when(step == last)
            def _():
                for f in range(5):
                    xlo[f, 0, ys, zc] += cx[px, 2 * cells] * low[f]
                    xhi[f, 0, ys, zc] += cx[px, 2 * cells + 2] * high[f]

        return 0

    lax.fori_loop(0, zs, piece, 0)

    @pl.when(step == last)
    def _():
        finish_ghosts(rows, coarse.shape[2], hg, sent, got, send_sem, recv_sem, groups, cells)


def lines_kernel(
    mx, my, mz, wz, sx, sy, sz, hg, to_low_x, to_high_x, to_low_y, to_high_y, rho, mom, ene,
    out, low_x, high_x, low_y, high_y, send_sem, recv_sem,
    f_buf, g_buf, h_buf, acc, mx_buf, my_buf, mz_buf, *, cells, tile, steps
):
    step = pl.program_id(0)
    width = rho.shape[2]
    zs = width // 128
    rows = tile * cells
    bf16 = jnp.bfloat16
    dot = functools.partial(jnp.dot, preferred_element_type=jnp.float32)
    chunks = [(z * 128, (z + 1) * 128) for z in range(zs)]

    moves = []
    for n, (axis, by, source, target) in enumerate(
        (("gx", 1, to_high_x, low_x), ("gx", -1, to_low_x, high_x),
         ("gy", 1, to_high_y, low_y), ("gy", -1, to_low_y, high_y))
    ):
        here, count = lax.axis_index(axis), lax.axis_size(axis)
        sends = here < count - 1 if by > 0 else here > 0
        gets = here > 0 if by > 0 else here < count - 1
        copy = pltpu.make_async_remote_copy(
            src_ref=source, dst_ref=target, send_sem=send_sem.at[n], recv_sem=recv_sem.at[n],
            device_id={axis: jnp.clip(here + by, 0, count - 1)}, device_id_type=pl.DeviceIdType.MESH,
        )
        moves.append((axis, here + by, sends, gets, copy))

    @pl.when(step == 0)
    def _():
        barrier = pltpu.get_barrier_semaphore()
        for axis, to, sends, _, _ in moves:
            @pl.when(sends)
            def _():
                pl.semaphore_signal(
                    barrier, inc=1, device_id={axis: to}, device_id_type=pl.DeviceIdType.MESH
                )
        pl.semaphore_wait(barrier, sum(jnp.where(gets, 1, 0) for _, _, _, gets, _ in moves))
        for _, _, sends, gets, copy in moves:
            @pl.when(sends)
            def _():
                copy.start()

        for buf, table in ((mx_buf, mx[lax.axis_index("gx")]), (my_buf, my[lax.axis_index("gy")])):
            buf[:, :rows] = table.astype(bf16)
            buf[:, rows:] = table.astype(bf16)
        mz_buf[...] = mz[...].astype(bf16)

    @pl.when(step < steps)
    def _():
        def piece(n, _):
            x = (n // (2 * zs)) * 2
            yy = pl.multiple_of((n // zs) % 2 * 16, 16)
            zc = pl.multiple_of((n % zs) * 128, 128)
            z_hi, z_lo = pl.ds(zc, 128), pl.ds(width + zc, 128)
            fields = load_fields(rho, mom, ene, (pl.ds(x, 2), pl.ds(yy, 16), z_hi))
            shared = common(fields)
            for f, value in enumerate(flux_from(fields, shared, 0)):
                for j in range(2):
                    hi, lo = split(value[:, 8 * j : 8 * j + 8].reshape(16, 128))
                    at = pl.multiple_of((step * tile + x) * 8, 16)
                    f_buf[yy // 8 + j, f, pl.ds(at, 16), z_hi] = hi
                    f_buf[yy // 8 + j, f, pl.ds(cells * 8 + at, 16), z_hi] = lo
            for f, value in enumerate(flux_from(fields, shared, 1)):
                for j in range(2):
                    hi, lo = split(value[j])
                    at = pl.multiple_of((x + j) * cells + yy, 16)
                    g_buf[f, pl.ds(at, 16), z_hi] = hi
                    g_buf[f, pl.ds(rows + at, 16), z_hi] = lo
            for f, value in enumerate(flux_from(fields, shared, 2)):
                for j in range(2):
                    hi, lo = split(value[j])
                    at = pl.multiple_of((x + j) * cells + yy, 16)
                    h_buf[f, pl.ds(at, 16), z_hi] = hi
                    h_buf[f, pl.ds(at, 16), z_lo] = lo
            return 0

        lax.fori_loop(0, (tile // 2) * 2 * zs, piece, 0)
        half = width // 2
        slots = hg.shape[2]
        own_slot = jnp.where(
            lax.broadcasted_iota(jnp.int32, (rows, slots), 1) % cells
            == lax.broadcasted_iota(jnp.int32, (rows, slots), 0) // cells + step * tile,
            1.0, 0.0,
        )
        for f in range(5):
            base = rho if f == 0 else ene if f == 4 else mom.at[f - 1]
            y_part = dot(my_buf[...], g_buf[f])
            g_hi, g_lo = split(jnp.concatenate([hg[f]] * tile, axis=0) * own_slot)
            ghost = jnp.concatenate([g_hi, g_lo], axis=1)
            for k in range(2):
                low = 0 if k == 0 else half - 128
                high = half + 128 if k == 0 else width
                left = jnp.concatenate([h_buf[f, :, low:high], h_buf[f, :, width + low : width + high]], axis=1)
                weight = mz_buf[low:high, k * half : (k + 1) * half]
                z_part = dot(left, jnp.concatenate([weight, weight], axis=0))
                edge = slice(0, 128) if k == 0 else slice(width - 128, width)
                ends = dot(ghost, wz[:, edge].astype(bf16))
                for a, b in chunks[k * zs // 2 : (k + 1) * zs // 2]:
                    got = z_part[:, a - k * half : b - k * half]
                    if a == edge.start:
                        got = got + ends
                    got = got * sz[:, a:b] + y_part[:, a:b] * sy[lax.axis_index("gy")]
                    acc[f, pl.ds(step * tile, tile), :, a:b] = base[:, :, a:b] + got.reshape(tile, cells, 128)

    @pl.when(step >= steps)
    def _():
        j = step - steps
        at = pl.multiple_of(j * 8, 8)
        for f in range(5):
            got = dot(mx_buf[...], f_buf[j, f])
            for a, b in chunks:
                part = (got[:, a:b] * sx[lax.axis_index("gx")]).reshape(cells, 8, 128)
                out[f, :, :, a:b] = acc[f, :, pl.ds(at, 8), a:b] + part

    @pl.when(step == 2 * steps - 1)
    def _():
        for _, _, sends, gets, copy in moves:
            @pl.when(sends)
            def _():
                copy.wait_send()

            @pl.when(gets)
            def _():
                copy.wait_recv()


def join_kernel(place, ax, ay, acc, xlo, xhi, ylo, yhi, out, *, cells, tile, last, groups, groups_y):
    step = pl.program_id(0)
    px, py = place[0], place[1]
    zs = acc.shape[3] // 128

    def piece(n, _):
        zc = pl.ds(pl.multiple_of(n * 128, 128), 128)
        weights = [(ax[px, step * tile + x], ax[px, cells + step * tile + x]) for x in range(tile)]
        for yy in range(0, cells, 8):
            ys = slice(yy, yy + 8)
            a_low, a_high = ay[0, 1, ys], ay[0, 3, ys]
            for f in range(5):
                x_low = jnp.where(px > 0, xlo[f, 1, ys, zc], 0.0)
                x_high = jnp.where(px < groups - 1, xhi[f, 1, ys, zc], 0.0)
                for x in range(tile):
                    row = slice(x, x + 1)
                    term = acc[f, x, ys, zc] + weights[x][0] * x_low + weights[x][1] * x_high
                    y_low = jnp.where(py > 0, ylo[f, 1, row, zc], 0.0)
                    y_high = jnp.where(py < groups_y - 1, yhi[f, 1, row, zc], 0.0)
                    term += a_low * y_low + a_high * y_high
                    if yy == 0:
                        term += ay[0, 0, ys] * jnp.where(py > 0, ylo[f, 0, row, zc], 0.0)
                    if yy + 8 == cells:
                        term += ay[0, 2, ys] * jnp.where(py < groups_y - 1, yhi[f, 0, row, zc], 0.0)
                    out[f, x, ys, zc] = term
        return 0

    lax.fori_loop(0, zs, piece, 0)

    @pl.when((step == 0) & (px > 0))
    def _():
        for f in range(5):
            out[f, 0] += xlo[f, 0]

    @pl.when((step == last) & (px < groups - 1))
    def _():
        for f in range(5):
            out[f, tile - 1] += xhi[f, 0]


def local(density, momentum, energy, coarse_rows, ghost_rows, time_index):
    cells, _, cells_z = density.shape
    groups_x, groups_y = lax.axis_size("gx"), lax.axis_size("gy")
    place_x, place_y = lax.axis_index("gx"), lax.axis_index("gy")
    place = jnp.stack([place_x, place_y]).astype(jnp.int32)
    tile = 8
    steps = cells // tile
    f32 = jnp.float32

    own_x, beyond_x, act_x = block_tables(cells, groups_x)
    own_y, beyond_y, act_y = block_tables(cells, groups_y)
    inverse_z, spread_z = line_matrices(cells_z)
    whole_z = -time_step * inverse_z @ spread_z
    at_x = np.tile(np.arange(cells), groups_x)
    at_y = np.tile(np.arange(cells), groups_y)
    scale_x, values_x = scaled_rows(own_x.reshape(-1, cells), at_x)
    scale_y, values_y = scaled_rows(own_y.reshape(-1, cells), at_y)
    scale_z, values_z = scaled_rows(whole_z, np.arange(cells_z) + 2)
    lanes = np.ones((1, 128), np.float32)
    mx = np.stack([np.kron(m, np.eye(8)) for m in values_x.reshape(own_x.shape)]).astype(np.float32)
    my = np.stack([np.kron(np.eye(tile), m) for m in values_y.reshape(own_y.shape)]).astype(np.float32)
    mz = np.ascontiguousarray(values_z[:, 2:-2].T)
    sx = np.stack([np.repeat(v, 8)[:, None] * lanes for v in scale_x.reshape(groups_x, cells)])
    sy = np.stack([np.tile(v, tile)[:, None] * lanes for v in scale_y.reshape(groups_y, cells)])
    sx, sy, sz = sx.astype(np.float32), sy.astype(np.float32), scale_z[None, :].astype(np.float32)
    wz = np.tile(np.repeat(values_z[:, [0, 1, cells_z + 2, cells_z + 3]].T, cells, axis=0), (2, 1))
    cy = edge_scalars(beyond_y, cells).astype(np.float32)
    weights = np.broadcast_to(beyond_y[:, 1::2, :, None], (groups_y, 2, cells, 128)).astype(np.float32)
    cx = edge_scalars(beyond_x, cells).astype(np.float32)
    ax = np.concatenate([act_x[:, 1], act_x[:, 3]], axis=1).astype(np.float32)
    ay = np.broadcast_to(act_y[..., None], act_y.shape + (128,)).astype(np.float32)


    smem = pl.BlockSpec(memory_space=pltpu.SMEM)
    anywhere = pl.BlockSpec(memory_space=pl.ANY)
    planes = jax.ShapeDtypeStruct((5, 2, cells, cells_z), f32)
    whole = jax.ShapeDtypeStruct((5, cells, cells, cells_z), f32)
    size = 4 * 5 * cells * cells * cells_z
    rows = tile * cells
    bf16 = jnp.bfloat16
    top = steps - 1

    def spec(dims, axis=None, index=lambda i: i):
        def place_of(i, *_):
            return tuple(index(i) if d == axis else 0 for d in range(len(dims)))

        return pl.BlockSpec(dims, place_of)

    def fixed(table):
        return spec(table.shape)

    def state_specs(index):
        return [
            spec((tile, cells, cells_z), 0, index),
            spec((3, tile, cells, cells_z), 1, index),
            spec((tile, cells, cells_z), 0, index),
        ]

    def params(**more):
        return pltpu.CompilerParams(
            vmem_limit_bytes=vmem_bytes, dimension_semantics=("arbitrary",), **more
        )

    def cost(flops, moved):
        return pl.CostEstimate(flops=flops, bytes_accessed=moved, transcendentals=0)

    slots, width = ghost_rows.shape[2], coarse_rows.shape[3]
    coarse = coarse_rows[:, :, 0, :].transpose(0, 2, 1)
    same = lambda i: i
    xlo, xhi, ylo, yhi, hg = pl.pallas_call(
        functools.partial(edge_kernel, cells=cells, tile=tile, last=top, groups=groups_x),
        grid=(steps,),
        in_specs=[
            smem, smem, fixed(weights), fixed(ghost_rows[0]), fixed(time_index[0]), fixed(coarse),
            *state_specs(same),
        ],
        out_shape=[planes] * 4 + [jax.ShapeDtypeStruct((5, cells, slots), f32)],
        out_specs=[
            spec(planes.shape), spec(planes.shape),
            spec((5, 2, tile, cells_z), 2), spec((5, 2, tile, cells_z), 2), spec((5, cells, slots)),
        ],
        scratch_shapes=[
            pltpu.VMEM((5, 2, tile, 8, 128), f32),
            pltpu.VMEM((slots, width), f32),
            pltpu.VMEM((slots, width), f32),
            pltpu.SemaphoreType.DMA((groups_x,)),
            pltpu.SemaphoreType.DMA((groups_x,)),
        ],
        compiler_params=params(collective_id=0, has_side_effects=True),
        cost_estimate=cost(size * 20, size),
        name="edges",
    )(cx, cy, weights, ghost_rows[0], time_index[0], coarse, density, momentum, energy)

    acc, in_xlo, in_xhi, in_ylo, in_yhi = pl.pallas_call(
        functools.partial(lines_kernel, cells=cells, tile=tile, steps=steps),
        grid=(2 * steps,),
        in_specs=[
            fixed(mx), fixed(my), fixed(mz), fixed(wz), fixed(sx), fixed(sy), fixed(sz), fixed(hg),
            *[anywhere] * 4, *state_specs(lambda i: jnp.minimum(i, top)),
        ],
        out_shape=[whole] + [planes] * 4,
        out_specs=[
            spec((5, cells, 8, cells_z), 2, lambda i: jnp.maximum(i - steps, 0)), *[anywhere] * 4
        ],
        scratch_shapes=[
            pltpu.SemaphoreType.DMA((4,)),
            pltpu.SemaphoreType.DMA((4,)),
            pltpu.VMEM((cells // 8, 5, 2 * cells * 8, cells_z), bf16),
            pltpu.VMEM((5, 2 * rows, cells_z), bf16),
            pltpu.VMEM((5, rows, 2 * cells_z), bf16),
            pltpu.VMEM((5, cells, cells, cells_z), f32),
            pltpu.VMEM((cells * 8, 2 * cells * 8), bf16),
            pltpu.VMEM((rows, 2 * rows), bf16),
            pltpu.VMEM((cells_z, cells_z), bf16),
        ],
        compiler_params=params(collective_id=1, has_side_effects=True),
        cost_estimate=cost(size * 1200, 2 * size),
        name="lines",
    )(mx, my, mz, wz, sx, sy, sz, hg, xlo, xhi, ylo, yhi, density, momentum, energy)

    return pl.pallas_call(
        functools.partial(join_kernel, cells=cells, tile=tile, last=top, groups=groups_x, groups_y=groups_y),
        grid_spec=pltpu.PrefetchScalarGridSpec(
            num_scalar_prefetch=1,
            grid=(steps,),
            in_specs=[
                smem, pl.BlockSpec((1, *ay.shape[1:]), lambda i, p: (p[1], 0, 0, 0)),
                spec((5, tile, cells, cells_z), 1), spec(planes.shape), spec(planes.shape),
                spec((5, 2, tile, cells_z), 2), spec((5, 2, tile, cells_z), 2),
            ],
            out_specs=spec((5, tile, cells, cells_z), 1),
        ),
        out_shape=whole,
        compiler_params=params(),
        cost_estimate=cost(size * 4, 2 * size),
        name="join",
    )(place, ax, ay, acc, in_xlo, in_xhi, in_ylo, in_yhi)


def solution(mesh):
    return jax.shard_map(
        local,
        mesh=mesh,
        in_specs=(
            P("gx", "gy", None),
            P(None, "gx", "gy", None),
            P("gx", "gy", None),
            P(None, "gx", "gy", None),
            P("gy", None, None),
            P("gy", None, None),
        ),
        out_specs=P(None, "gx", "gy", None),
        check_vma=False,
    )
```
